32 devices in a mesh: tm: 8 (over z, y), col: 4 (over x, core).
Axes of the slice: x: 2, y: 2, z: 4, core: 2. Of those that a mesh axis runs over, the one named last changes fastest.
Arguments:
- transition: bfloat16 [64, 256, 256], P('tm', 'col'), may hold values from -1 to 1, as said below
- drive: float32 [64, 16, 256], P('tm', 'col'), may hold values from -0.3125 to 0.3125
- smoother_gain: bfloat16 [64, 256, 256], P('tm', 'col'), may hold values from -1 to 1, as said below
- dynamics: float32 [256, 256], replicated, may hold values from -0.375 to 0.375
- initial_mean: float32 [16, 256], P('col'), may hold values from -6 to 6
Outputs:
- filtered_mean: float32 [64, 16, 256], P('tm', 'col')
- smoothed_mean: float32 [64, 16, 256], P('tm', 'col')
The draws below stay inside these ranges and needn't reach their ends.
Inputs may be any that keep to these rules, and one draw needn't show every extreme that they name: `transition`: every step operator is a per-channel diagonal plus a dense full-rank part. `smoother_gain`: every gain is a per-channel diagonal plus a dense full-rank part.
All inputs are finite; a program needn't handle non-finite values.
Results may differ from the reference program's by a relative error of at most 0.0018.
Values may be sent and summed in bfloat16 or wider, within the bound.
A program may use at most 128 MiB of HBM per device.

```python
import jax
import jax.numpy as jnp
from jax import lax

D = 256
TIME_STEP_COUNT = 64
SERIES = 16


def operator_draw(key, salt):
    baseline_level = jax.random.fold_in(key, salt)
    arrival_rate_key, jitter_noise_key, spike_event_key = jax.random.split(baseline_level, 3)
    rates = 0.85 + 0.14 * jax.random.uniform(arrival_rate_key, (D,), jnp.float32)
    noise = jax.random.normal(jitter_noise_key, (TIME_STEP_COUNT, D, D), jnp.float32)
    spike_events = jax.random.randint(spike_event_key, (4,), 0, TIME_STEP_COUNT)
    step_values = jnp.arange(TIME_STEP_COUNT)
    spike_hits = jnp.any(step_values[:, None] == spike_events[None, :], axis=1)
    diagonal = rates[None, :] * jnp.where(spike_hits, 0.6, 1.0)[:, None]
    ident = jnp.eye(D, dtype=jnp.float32)
    result = noise * (0.39 * D ** (-0.5)) + ident[None, :, :] * diagonal[:, None, :]
    return jnp.clip(result, -1.0, 1.0)


def draw_transition(key, part):
    return operator_draw(key, 11).astype(jnp.bfloat16)


def draw_smoother_gain(key, part):
    return operator_draw(key, 23).astype(jnp.bfloat16)


def shard_levels(key, dims, pieces, low, high):
    def one(dim, parts):
        draws = jax.random.uniform(jax.random.fold_in(jax.random.fold_in(key, 6), dim), (parts,), jnp.float32, low / len(pieces), high / len(pieces))
        return jnp.repeat(jnp.exp(draws), dims[dim] // parts).reshape((-1,) + (1,) * (len(dims) - dim - 1))

    level = one(*pieces[0])
    for cut in pieces[1:]:
        level = level * one(*cut)
    return level


def scatter_about(key, dims, scale, reach, cuts=(), held_as=jnp.bfloat16):
    drawn = scale * jax.random.normal(key, dims, jnp.float32)
    if cuts:
        drawn = drawn * shard_levels(key, dims, cuts, -0.22, 0.18)
    return jnp.clip(drawn, -reach, reach).astype(held_as)


def setup_inputs(seed: int = 0) -> dict:
    streams_of = jax.random.split(jax.random.key(seed), 6)
    return {
        "transition": draw_transition(jax.random.fold_in(streams_of[5], 71), 0),
        "drive": scatter_about(streams_of[1], (TIME_STEP_COUNT, SERIES, D), 0.05, 0.3125, ((0, 8), (1, 4)), jnp.float32),
        "smoother_gain": draw_smoother_gain(jax.random.fold_in(streams_of[5], 71), 0),
        "dynamics": scatter_about(streams_of[3], (D, D), D ** -0.5, 0.375, (), jnp.float32),
        "initial_mean": scatter_about(streams_of[4], (SERIES, D), 1.0, 6.0, ((0, 4),), jnp.float32),
    }


highest = lax.Precision.HIGHEST


def reference(transition, drive, smoother_gain, dynamics, initial_mean):
    positions = jnp.arange(TIME_STEP_COUNT)
    keep = positions < TIME_STEP_COUNT - 1
    gains = jnp.where(keep[:, None, None], smoother_gain, jnp.zeros_like(smoother_gain))

    def forward_step(state, inputs):
        operator, push = inputs
        state = jnp.dot(state, operator.astype(jnp.float32), precision=highest, preferred_element_type=jnp.float32) + push
        return state, state

    _, filtered = lax.scan(forward_step, initial_mean.astype(jnp.float32), (transition, drive))

    def correct_step(carry, inputs):
        mean_now, gain_now = inputs
        projected = jnp.dot(mean_now, dynamics, precision=highest, preferred_element_type=jnp.float32)
        result = mean_now - jnp.dot(projected, gain_now.astype(jnp.float32), precision=highest, preferred_element_type=jnp.float32)
        return carry, result

    _, correction = lax.scan(correct_step, jnp.float32(0.0), (filtered, gains))

    def backward_step(state, inputs):
        gain_now, corr_now = inputs
        state = jnp.dot(state, gain_now.astype(jnp.float32), precision=highest, preferred_element_type=jnp.float32) + corr_now
        return state, state

    begin = jnp.zeros((SERIES, D), jnp.float32)
    _, smoothed = lax.scan(backward_step, begin, (gains, correction), reverse=True)
    return filtered, smoothed
```

```python
import functools

import jax
import jax.numpy as jnp
from jax import lax
from jax.experimental import pallas as pl
from jax.experimental.pallas import tpu as pltpu
from jax.sharding import PartitionSpec as P

MESH = pl.DeviceIdType.MESH
PAD = 8


def dot(left, right):
    return jnp.dot(left, right, preferred_element_type=jnp.float32)


def halves(x):
    hi = x.astype(jnp.bfloat16)
    lo = (x - hi.astype(jnp.float32)).astype(jnp.bfloat16)
    return hi, lo


def stacked(x):
    hi = x.astype(jnp.bfloat16).astype(jnp.float32)
    return jnp.concatenate([hi, x - hi], axis=0).astype(jnp.bfloat16)


def folded(r):
    rows = r.shape[0] // 2
    return r[:rows] + r[rows:]


def kernel(
    blocks, steps, rows, series,
    a_ref, g_ref, drive_ref, dyn_ref, init_ref, filt_ref, smooth_ref,
    a_full, g_full, a_pre, g_pre, vst, fst, lst, pst, dyn_hl, x_out, x_in, s_out, s_in,
    local_sem, send_sem, recv_sem, chain_send, chain_recv,
):
    dim = dyn_ref.shape[0]
    place = lax.axis_index("tm")
    me = lax.axis_index("col")
    sib = me + 1 - 2 * lax.rem(me, 2)
    cross = lax.rem(me + 2, 4)
    first = place == 0
    last = place == blocks - 1

    barrier = pltpu.get_barrier_semaphore()
    for other in (sib, cross):
        pl.semaphore_signal(barrier, inc=1, device_id={"col": other}, device_id_type=MESH)

    @pl.when(jnp.logical_not(first))
    def _():
        pl.semaphore_signal(barrier, inc=1, device_id={"tm": place - 1}, device_id_type=MESH)

    @pl.when(jnp.logical_not(last))
    def _():
        pl.semaphore_signal(barrier, inc=1, device_id={"tm": place + 1}, device_id_type=MESH)

    neighbours = 4 - jnp.where(first, 1, 0) - jnp.where(last, 1, 0)
    pl.semaphore_wait(barrier, neighbours)

    own = pl.ds(pl.multiple_of(me * rows, rows), rows)
    passed = pl.ds(pl.multiple_of(cross * rows, rows), rows)

    def move(which, kind, t):
        source, full = ((a_ref, a_full), (g_ref, g_full))[which]
        if kind == 2:
            src = full.at[t, passed, :]
            dst = full.at[t, passed, :]
        else:
            src = source.at[t]
            dst = full.at[t, own, :]
        return pltpu.make_async_remote_copy(
            src_ref=src,
            dst_ref=dst,
            send_sem=send_sem.at[which, kind, t],
            recv_sem=recv_sem.at[which, kind, t],
            device_id={"col": cross if kind == 1 else sib},
            device_id_type=MESH,
        )

    def kept(which):
        source, full = ((a_ref, a_full), (g_ref, g_full))[which]
        return pltpu.make_async_copy(source, full.at[:, own, :], local_sem.at[which])

    for t in range(steps):
        move(0, 1, t).start()
    for t in range(steps):
        move(0, 0, t).start()
    kept(0).start()

    hi, lo = halves(dyn_ref[...])
    dyn_hl[0] = hi
    dyn_hl[1] = lo
    rest = jnp.zeros((PAD - series, dim), jnp.float32)

    def padded(x):
        return jnp.concatenate([x, rest], axis=0)

    def pass_on(which, t):
        move(which, 1, t).wait_recv()
        move(which, 2, t).start()

    def keep_pre(pre, t, p):
        hi, lo = halves(p)
        pre[t, 0:dim] = hi
        pre[t, dim : 2 * dim] = lo

    kept(0).wait()
    ahead = 2
    for t in range(ahead):
        pass_on(0, t)

    def arrived(which, t):
        move(which, 0, t).wait_recv()
        move(which, 2, t).wait_recv()

    arrived(0, 0)
    a_pre[0, 0:dim] = a_full[0]
    a_pre[0, dim : 2 * dim] = jnp.zeros((dim, dim), jnp.bfloat16)
    v0 = padded(drive_ref[0])
    vst[0] = v0
    a_pre[0, 2 * dim : 2 * dim + 2 * PAD] = stacked(v0)

    def forward_step(t, carry):
        @pl.when(t + ahead - 1 < steps)
        def _():
            pass_on(0, t + ahead - 1)

        arrived(0, t)
        r = dot(a_pre[t - 1], a_full[t])
        v = folded(r[2 * dim :]) + padded(drive_ref[t])
        keep_pre(a_pre, t, r[0:dim] + r[dim : 2 * dim])
        vst[t] = v
        a_pre[t, 2 * dim : 2 * dim + 2 * PAD] = stacked(v)
        return carry

    lax.fori_loop(1, steps, forward_step, 0)

    for t in reversed(range(steps)):
        move(1, 1, t).start()
    for t in reversed(range(steps)):
        move(1, 0, t).start()
    kept(1).start()

    late = place >= blocks // 2

    def pass_gains():
        for t in reversed(range(steps)):
            pass_on(1, t)

    pl.when(late)(pass_gains)

    def chain(way):
        src, dst = ((x_out, x_in), (s_out, s_in))[way]
        return pltpu.make_async_remote_copy(
            src_ref=src,
            dst_ref=dst,
            send_sem=chain_send.at[way],
            recv_sem=chain_recv.at[way],
            device_id={"tm": place + 1 if way == 0 else place - 1},
            device_id_type=MESH,
        )

    @pl.when(first)
    def _():
        x_in[...] = padded(init_ref[...])

    @pl.when(jnp.logical_not(first))
    def _():
        chain(0).wait_recv()

    x = stacked(x_in[...])

    def filtered_at(t):
        r = dot(x, a_pre[t, 0:dim]) + dot(x, a_pre[t, dim : 2 * dim])
        f = folded(r) + vst[t]
        fst[t * PAD : (t + 1) * PAD] = f
        filt_ref[t] = f[0:series]
        return f

    x_out[...] = filtered_at(steps - 1)

    @pl.when(jnp.logical_not(last))
    def _():
        chain(0).start()

    for t in range(steps - 1):
        filtered_at(t)

    pl.when(jnp.logical_not(late))(pass_gains)

    f_all = stacked(fst[...])
    pst[...] = folded(dot(f_all, dyn_hl[0]) + dot(f_all, dyn_hl[1]))
    kept(1).wait()

    end = steps - 1

    def rows_of(t):
        return pl.ds(pl.multiple_of(t * PAD, PAD), PAD)

    arrived(1, end)

    @pl.when(last)
    def _():
        lst[end] = fst[rows_of(end)]

        def only_means(lap, state):
            t = end - lap
            arrived(1, t)
            now = folded(dot(stacked(state - pst[rows_of(t)]), g_full[t])) + fst[rows_of(t)]
            lst[t] = now
            return now

        lax.fori_loop(1, steps, only_means, fst[rows_of(end)])
        s_out[...] = lst[0]
        chain(1).start()
        for t in range(steps):
            smooth_ref[t] = lst[t][0:series]

    @pl.when(jnp.logical_not(last))
    def _():
        g_pre[end, 0:dim] = g_full[end]
        g_pre[end, dim : 2 * dim] = jnp.zeros((dim, dim), jnp.bfloat16)
        now = folded(dot(stacked(-pst[rows_of(end)]), g_full[end])) + fst[rows_of(end)]
        lst[end] = now
        g_pre[end, 2 * dim :] = stacked(now - pst[rows_of(end - 1)])

        def backward_step(lap, carry):
            t = end - lap
            arrived(1, t)
            r = dot(g_pre[t + 1], g_full[t])
            keep_pre(g_pre, t, r[0:dim] + r[dim : 2 * dim])
            now = folded(r[2 * dim :]) + fst[rows_of(t)]
            lst[t] = now
            below = jnp.maximum(t - 1, 0)
            g_pre[t, 2 * dim :] = stacked(now - pst[rows_of(below)])
            return carry

        lax.fori_loop(1, steps, backward_step, 0)

        chain(1).wait_recv()
        s = stacked(s_in[...])

        def smoothed_at(t):
            r = dot(s, g_pre[t, 0:dim]) + dot(s, g_pre[t, dim : 2 * dim])
            now = folded(r) + lst[t]
            smooth_ref[t] = now[0:series]
            return now

        s_out[...] = smoothed_at(0)

        @pl.when(jnp.logical_not(first))
        def _():
            chain(1).start()

        for t in range(1, steps):
            smoothed_at(t)

    def sent(t, carry):
        for which in range(2):
            for kind in range(3):
                move(which, kind, t).wait_send()
        return carry

    lax.fori_loop(0, steps, sent, 0)

    @pl.when(jnp.logical_not(last))
    def _():
        chain(0).wait_send()

    @pl.when(jnp.logical_not(first))
    def _():
        chain(1).wait_send()


def local(blocks, transition, drive, smoother_gain, dynamics, initial_mean):
    steps, rows, dim = transition.shape
    series = initial_mean.shape[0]
    vmem = pl.BlockSpec(memory_space=pltpu.VMEM)
    hbm = pl.BlockSpec(memory_space=pl.ANY)
    full = pltpu.VMEM((steps, dim, dim), jnp.bfloat16)
    pre = pltpu.VMEM((steps, 2 * dim + 2 * PAD, dim), jnp.bfloat16)
    means = pltpu.VMEM((steps, PAD, dim), jnp.float32)
    flat = pltpu.VMEM((steps * PAD, dim), jnp.float32)
    one = pltpu.VMEM((PAD, dim), jnp.float32)
    out = jax.ShapeDtypeStruct(drive.shape, jnp.float32)
    return pl.pallas_call(
        functools.partial(kernel, blocks, steps, rows, series),
        out_shape=(out, out),
        in_specs=[hbm, hbm, vmem, vmem, vmem],
        out_specs=(vmem, vmem),
        scratch_shapes=[
            full, full, pre, pre, means, flat, means, flat,
            pltpu.VMEM((2, dim, dim), jnp.bfloat16),
            one, one, one, one,
            pltpu.SemaphoreType.DMA((2,)),
            pltpu.SemaphoreType.DMA((2, 3, steps)),
            pltpu.SemaphoreType.DMA((2, 3, steps)),
            pltpu.SemaphoreType.DMA((2,)),
            pltpu.SemaphoreType.DMA((2,)),
        ],
        compiler_params=pltpu.CompilerParams(
            collective_id=0, has_side_effects=True, vmem_limit_bytes=40 * 1024 * 1024
        ),
    )(transition, smoother_gain, drive, dynamics, initial_mean)


def solution(mesh):
    placed = (P("tm", "col", None), P("tm", "col", None), P("tm", "col", None), P(), P("col", None))
    return jax.shard_map(
        functools.partial(local, mesh.shape["tm"]),
        mesh=mesh,
        in_specs=placed,
        out_specs=(P("tm", "col", None), P("tm", "col", None)),
        check_vma=False,
    )
```

```python
import functools

import jax
import jax.numpy as jnp
from jax import lax
from jax.experimental import pallas as pl
from jax.experimental.pallas import tpu as pltpu
from jax.sharding import PartitionSpec as P

MESH = pl.DeviceIdType.MESH
PAD = 8
GROUP = 4


def dot(left, right):
    return jnp.dot(left, right, preferred_element_type=jnp.float32)


def halves(x):
    hi = x.astype(jnp.bfloat16)
    lo = (x - hi.astype(jnp.float32)).astype(jnp.bfloat16)
    return hi, lo


def stacked(x):
    hi = x.astype(jnp.bfloat16).astype(jnp.float32)
    return jnp.concatenate([hi, x - hi], axis=0).astype(jnp.bfloat16)


def folded(r):
    rows = r.shape[0] // 2
    return r[:rows] + r[rows:]


def kernel(
    blocks, steps, rows, series,
    a_ref, g_ref, drive_hbm, dyn_hbm, init_hbm, filt_ref, smooth_ref,
    drive_ref, dyn_ref, init_ref,
    a_full, g_full, a_pre, g_pre, a_got, g_got, v_got, b_got, v_out, b_out,
    vst, fst, lst, pst, dyn_hl, x_out, x_in, s_out, s_in,
    local_sem, send_sem, recv_sem, group_send, group_recv, chain_send, chain_recv,
):
    dim = dyn_ref.shape[0]

    def fetch(n):
        src, dst = ((drive_hbm, drive_ref), (dyn_hbm, dyn_ref), (init_hbm, init_ref))[n]
        return pltpu.make_async_copy(src, dst, local_sem.at[2 + n])

    for n in range(3):
        fetch(n).start()
    place = lax.axis_index("tm")
    me = lax.axis_index("col")
    sib = me + 1 - 2 * lax.rem(me, 2)
    cross = lax.rem(me + 2, 4)
    q = lax.rem(place, GROUP)
    begin = place - q
    first = place == 0
    last = place == blocks - 1
    low = begin == 0
    high = begin == blocks - GROUP

    barrier = pltpu.get_barrier_semaphore()

    def greet(other):
        pl.semaphore_signal(barrier, inc=1, device_id=other, device_id_type=MESH)

    greet({"col": sib})
    greet({"col": cross})
    for d in range(1, GROUP):
        greet({"tm": begin + lax.rem(q + d, GROUP)})

    @pl.when(jnp.logical_not(high))
    def _():
        greet({"tm": begin + GROUP})

        @pl.when(q == GROUP - 1)
        def _():
            for d in range(1, GROUP):
                greet({"tm": begin + GROUP + d})

    @pl.when(jnp.logical_not(low))
    def _():
        greet({"tm": begin - 1})

        @pl.when(q == 0)
        def _():
            for d in range(1, GROUP):
                greet({"tm": begin - 1 - d})

    above = jnp.where(high, 0, jnp.where(q == GROUP - 1, GROUP, 1))
    below = jnp.where(low, 0, jnp.where(q == 0, GROUP, 1))
    pl.semaphore_wait(barrier, GROUP + 1 + above + below)

    own = pl.ds(pl.multiple_of(me * rows, rows), rows)
    passed = pl.ds(pl.multiple_of(cross * rows, rows), rows)

    def move(which, kind, t):
        source, full = ((a_ref, a_full), (g_ref, g_full))[which]
        if kind == 2:
            src = full.at[t, passed, :]
            dst = full.at[t, passed, :]
        else:
            src = source.at[t]
            dst = full.at[t, own, :]
        return pltpu.make_async_remote_copy(
            src_ref=src,
            dst_ref=dst,
            send_sem=send_sem.at[which, kind, t],
            recv_sem=recv_sem.at[which, kind, t],
            device_id={"col": cross if kind == 1 else sib},
            device_id_type=MESH,
        )

    def kept(which):
        source, full = ((a_ref, a_full), (g_ref, g_full))[which]
        return pltpu.make_async_copy(source, full.at[:, own, :], local_sem.at[which])

    for t in range(steps):
        move(0, 1, t).start()
    for t in range(steps):
        move(0, 0, t).start()
    kept(0).start()

    for n in range(3):
        fetch(n).wait()

    hi, lo = halves(dyn_ref[...])
    dyn_hl[0] = hi
    dyn_hl[1] = lo
    rest = jnp.zeros((PAD - series, dim), jnp.float32)

    def padded(x):
        return jnp.concatenate([x, rest], axis=0)

    def pass_on(which, t):
        move(which, 1, t).wait_recv()
        move(which, 2, t).start()

    def keep_pre(pre, t, p):
        hi, lo = halves(p)
        pre[t, 0:dim] = hi
        pre[t, dim : 2 * dim] = lo

    kept(0).wait()
    ahead = 2
    for t in range(ahead):
        pass_on(0, t)

    def arrived(which, t):
        move(which, 0, t).wait_recv()
        move(which, 2, t).wait_recv()

    arrived(0, 0)
    a_pre[0, 0:dim] = a_full[0]
    a_pre[0, dim : 2 * dim] = jnp.zeros((dim, dim), jnp.bfloat16)
    v0 = padded(drive_ref[0])
    vst[0] = v0
    a_pre[0, 2 * dim : 2 * dim + 2 * PAD] = stacked(v0)

    def forward_step(t, carry):
        @pl.when(t + ahead - 1 < steps)
        def _():
            pass_on(0, t + ahead - 1)

        arrived(0, t)
        r = dot(a_pre[t - 1], a_full[t])
        v = folded(r[2 * dim :]) + padded(drive_ref[t])
        keep_pre(a_pre, t, r[0:dim] + r[dim : 2 * dim])
        vst[t] = v
        a_pre[t, 2 * dim : 2 * dim + 2 * PAD] = stacked(v)
        return carry

    lax.fori_loop(1, steps, forward_step, 0)

    for t in reversed(range(steps)):
        move(1, 1, t).start()
    for t in reversed(range(steps)):
        move(1, 0, t).start()
    kept(1).start()

    half = lax.rem(me, 2)
    mine = pl.ds(pl.multiple_of(half * dim, dim), dim)

    def group_copy(way, kind, slot, d):
        pre, got, out, means = ((a_pre, a_got, v_out, v_got), (g_pre, g_got, b_out, b_got))[way]
        block = steps - 1 if way == 0 else 0
        if kind == 0:
            src, dst = pre.at[block, mine, :], got.at[slot, mine, :]
        elif kind == 1:
            src, dst = out, means.at[slot]
        else:
            src, dst = got.at[slot, mine, :], got.at[slot, mine, :]
        to = {"col": sib} if kind == 2 else {"tm": place + d if way == 0 else place - d}
        return pltpu.make_async_remote_copy(
            src_ref=src,
            dst_ref=dst,
            send_sem=group_send.at[way, kind, slot if kind == 2 else d - 1],
            recv_sem=group_recv.at[way, kind, slot],
            device_id=to,
            device_id_type=MESH,
        )

    def each_target(way, body):
        for d in reversed(range(1, GROUP)):
            pl.when(q + d <= GROUP - 1 if way == 0 else q >= d)(functools.partial(body, d))

    def spread(way, kind):
        slot = q if way == 0 else q - 1
        each_target(way, lambda d: group_copy(way, kind, slot, d).start())

    def each_source(way, body):
        for s in range(GROUP - 1) if way == 0 else reversed(range(GROUP - 1)):
            pl.when(q > s if way == 0 else q <= s)(functools.partial(body, s))

    def share(way):
        def one(s):
            group_copy(way, 0, s, 1).wait_recv()
            group_copy(way, 2, s, 1).start()

        if way == 0:
            each_source(way, one)
        else:
            for s in reversed(range(GROUP - 1)):
                there = jnp.logical_and(q <= s, jnp.logical_not(jnp.logical_and(high, s == GROUP - 2)))
                pl.when(there)(functools.partial(one, s))

    v_out[...] = vst[steps - 1]
    spread(0, 0)
    spread(0, 1)

    end = steps - 1

    def rows_of(t):
        return pl.ds(pl.multiple_of(t * PAD, PAD), PAD)

    def gains():
        for t in reversed(range(steps)):
            pass_on(1, t)
        kept(1).wait()
        arrived(1, end)

        @pl.when(jnp.logical_not(last))
        def _():
            g_pre[end, 0:dim] = g_full[end]
            g_pre[end, dim : 2 * dim] = jnp.zeros((dim, dim), jnp.bfloat16)

            def gain_step(lap, carry):
                t = end - lap
                arrived(1, t)
                r = dot(g_pre[t + 1], g_full[t])
                keep_pre(g_pre, t, r[0:dim] + r[dim : 2 * dim])
                return carry

            lax.fori_loop(1, steps, gain_step, 0)
            spread(1, 0)

        @pl.when(last)
        def _():
            def only_wait(lap, carry):
                arrived(1, end - lap)
                return carry

            lax.fori_loop(1, steps, only_wait, 0)

    share(0)
    pl.when(jnp.logical_not(low))(gains)

    def chain(way, d):
        src, dst = ((x_out, x_in), (s_out, s_in))[way]
        return pltpu.make_async_remote_copy(
            src_ref=src,
            dst_ref=dst,
            send_sem=chain_send.at[way, d - 1],
            recv_sem=chain_recv.at[way],
            device_id={"tm": place + d if way == 0 else place - d},
            device_id_type=MESH,
        )

    def applied(state, pre, block):
        r = dot(state, pre[block, 0:dim]) + dot(state, pre[block, dim : 2 * dim])
        return folded(r)

    @pl.when(low)
    def _():
        x_in[...] = padded(init_ref[...])

    @pl.when(jnp.logical_not(low))
    def _():
        chain(0, 1).wait_recv()

    def take(s):
        group_copy(0, 2, s, 1).wait_recv()
        group_copy(0, 1, s, 1).wait_recv()
        x_in[...] = applied(stacked(x_in[...]), a_got, s) + v_got[s]

    each_source(0, take)
    x = stacked(x_in[...])

    def filtered_at(t):
        f = applied(x, a_pre, t) + vst[t]
        fst[t * PAD : (t + 1) * PAD] = f
        filt_ref[t] = f[0:series]
        return f

    x_out[...] = filtered_at(end)
    gives = jnp.logical_and(q == GROUP - 1, jnp.logical_not(high))

    @pl.when(gives)
    def _():
        for d in reversed(range(1, GROUP + 1)):
            chain(0, d).start()

    for t in range(end):
        filtered_at(t)

    pl.when(low)(gains)

    f_all = stacked(fst[...])
    pst[...] = folded(dot(f_all, dyn_hl[0]) + dot(f_all, dyn_hl[1]))

    def mean_step(state, t):
        now = folded(dot(stacked(state - pst[rows_of(t)]), g_full[t])) + fst[rows_of(t)]
        lst[t] = now
        return now

    @pl.when(last)
    def _():
        lst[end] = fst[rows_of(end)]

    @pl.when(jnp.logical_not(last))
    def _():
        mean_step(jnp.zeros((PAD, dim), jnp.float32), end)

    state = lst[end]
    for t in reversed(range(end)):
        state = mean_step(state, t)
    b_out[...] = state
    spread(1, 1)
    share(1)

    @pl.when(high)
    def _():
        s_in[...] = jnp.zeros((PAD, dim), jnp.float32)

    @pl.when(jnp.logical_not(high))
    def _():
        chain(1, 1).wait_recv()

    def take_back(s):
        group_copy(1, 1, s, 1).wait_recv()

        def product():
            group_copy(1, 2, s, 1).wait_recv()
            s_in[...] = applied(stacked(s_in[...]), g_got, s) + b_got[s]

        if s == GROUP - 2:
            pl.when(jnp.logical_not(high))(product)

            @pl.when(high)
            def _():
                s_in[...] = b_got[s]
        else:
            product()

    each_source(1, take_back)

    @pl.when(last)
    def _():
        s_out[...] = lst[0]
        for t in range(steps):
            smooth_ref[t] = lst[t][0:series]

    returns = jnp.logical_and(q == 0, jnp.logical_not(low))

    @pl.when(jnp.logical_not(last))
    def _():
        s = stacked(s_in[...])

        def smoothed_at(t):
            now = applied(s, g_pre, t) + lst[t]
            smooth_ref[t] = now[0:series]
            return now

        s_out[...] = smoothed_at(0)

        @pl.when(returns)
        def _():
            for d in reversed(range(1, GROUP + 1)):
                chain(1, d).start()

        for t in range(1, steps):
            smoothed_at(t)

    def sent(t, carry):
        for which in range(2):
            for kind in range(3):
                move(which, kind, t).wait_send()
        return carry

    lax.fori_loop(0, steps, sent, 0)

    for way in range(2):
        for kind in range(2):
            def done(d, way=way, kind=kind):
                group_copy(way, kind, 0, d).wait_send()

            if way == 1 and kind == 0:
                pl.when(jnp.logical_not(last))(lambda: each_target(way, done))
            else:
                each_target(way, done)

    def shared(way, s):
        group_copy(way, 2, s, 1).wait_send()

    each_source(0, functools.partial(shared, 0))
    for s in range(GROUP - 1):
        there = jnp.logical_and(q <= s, jnp.logical_not(jnp.logical_and(high, s == GROUP - 2)))
        pl.when(there)(functools.partial(shared, 1, s))

    for way, sender in ((0, gives), (1, returns)):
        @pl.when(sender)
        def _():
            for d in range(1, GROUP + 1):
                chain(way, d).wait_send()


def local(blocks, transition, drive, smoother_gain, dynamics, initial_mean):
    steps, rows, dim = transition.shape
    series = initial_mean.shape[0]
    vmem = pl.BlockSpec(memory_space=pltpu.VMEM)
    hbm = pl.BlockSpec(memory_space=pltpu.HBM)
    full = pltpu.VMEM((steps, dim, dim), jnp.bfloat16)
    a_pre = pltpu.VMEM((steps, 2 * dim + 2 * PAD, dim), jnp.bfloat16)
    g_pre = pltpu.VMEM((steps, 2 * dim, dim), jnp.bfloat16)
    got = pltpu.VMEM((GROUP - 1, 2 * dim, dim), jnp.bfloat16)
    group = pltpu.VMEM((GROUP - 1, PAD, dim), jnp.float32)
    means = pltpu.VMEM((steps, PAD, dim), jnp.float32)
    flat = pltpu.VMEM((steps * PAD, dim), jnp.float32)
    one = pltpu.VMEM((PAD, dim), jnp.float32)
    out = jax.ShapeDtypeStruct(drive.shape, jnp.float32)
    return pl.pallas_call(
        functools.partial(kernel, blocks, steps, rows, series),
        out_shape=(out, out),
        in_specs=[hbm] * 5,
        out_specs=(vmem, vmem),
        scratch_shapes=[
            pltpu.VMEM(drive.shape, drive.dtype),
            pltpu.VMEM(dynamics.shape, dynamics.dtype),
            pltpu.VMEM(initial_mean.shape, initial_mean.dtype),
            full, full, a_pre, g_pre, got, got, group, group, one, one,
            means, flat, means, flat,
            pltpu.VMEM((2, dim, dim), jnp.bfloat16),
            one, one, one, one,
            pltpu.SemaphoreType.DMA((5,)),
            pltpu.SemaphoreType.DMA((2, 3, steps)),
            pltpu.SemaphoreType.DMA((2, 3, steps)),
            pltpu.SemaphoreType.DMA((2, 3, GROUP - 1)),
            pltpu.SemaphoreType.DMA((2, 3, GROUP - 1)),
            pltpu.SemaphoreType.DMA((2, GROUP)),
            pltpu.SemaphoreType.DMA((2,)),
        ],
        compiler_params=pltpu.CompilerParams(
            collective_id=0, has_side_effects=True, vmem_limit_bytes=60 * 1024 * 1024
        ),
    )(transition, smoother_gain, drive, dynamics, initial_mean)


def solution(mesh):
    placed = (P("tm", "col", None), P("tm", "col", None), P("tm", "col", None), P(), P("col", None))
    return jax.shard_map(
        functools.partial(local, mesh.shape["tm"]),
        mesh=mesh,
        in_specs=placed,
        out_specs=(P("tm", "col", None), P("tm", "col", None)),
        check_vma=False,
    )
```

```python
import functools

import jax
import jax.numpy as jnp
from jax import lax
from jax.experimental import pallas as pl
from jax.experimental.pallas import tpu as pltpu
from jax.sharding import PartitionSpec as P

MESH = pl.DeviceIdType.MESH
PAD = 8
GROUP = 4


def dot(left, right):
    return jnp.dot(left, right, preferred_element_type=jnp.float32)


def halves(x):
    hi = x.astype(jnp.bfloat16)
    lo = (x - hi.astype(jnp.float32)).astype(jnp.bfloat16)
    return hi, lo


def stacked(x):
    hi = x.astype(jnp.bfloat16).astype(jnp.float32)
    return jnp.concatenate([hi, x - hi], axis=0).astype(jnp.bfloat16)


def folded(r):
    rows = r.shape[0] // 2
    return r[:rows] + r[rows:]


def kernel(
    blocks, steps, rows, series,
    a_ref, g_ref, drive_hbm, dyn_hbm, init_hbm, filt_ref, smooth_ref,
    drive_ref, dyn_ref, init_ref,
    a_full, g_full, a_pre, g_pre, a_got, g_got, v_got, b_got, v_out, b_out,
    vst, fst, lst, pst, dyn_hl, x_out, x_in, s_out, s_in,
    local_sem, send_sem, recv_sem, group_send, group_recv, chain_send, chain_recv,
):
    dim = dyn_ref.shape[0]

    def fetch(n):
        src, dst = ((drive_hbm, drive_ref), (dyn_hbm, dyn_ref), (init_hbm, init_ref))[n]
        return pltpu.make_async_copy(src, dst, local_sem.at[2 + n])

    for n in range(3):
        fetch(n).start()
    place = lax.axis_index("tm")
    me = lax.axis_index("col")
    sib = me + 1 - 2 * lax.rem(me, 2)
    cross = lax.rem(me + 2, 4)
    q = lax.rem(place, GROUP)
    begin = place - q
    first = place == 0
    last = place == blocks - 1
    low = begin == 0
    high = begin == blocks - GROUP

    barrier = pltpu.get_barrier_semaphore()

    def greet(other):
        pl.semaphore_signal(barrier, inc=1, device_id=other, device_id_type=MESH)

    greet({"col": sib})
    greet({"col": cross})
    for d in range(1, GROUP):
        greet({"tm": begin + lax.rem(q + d, GROUP)})

    @pl.when(jnp.logical_not(high))
    def _():
        greet({"tm": begin + GROUP})

        @pl.when(q == GROUP - 1)
        def _():
            for d in range(1, GROUP):
                greet({"tm": begin + GROUP + d})

    @pl.when(jnp.logical_not(low))
    def _():
        greet({"tm": begin - 1})

        @pl.when(q == 0)
        def _():
            for d in range(1, GROUP):
                greet({"tm": begin - 1 - d})

    above = jnp.where(high, 0, jnp.where(q == GROUP - 1, GROUP, 1))
    below = jnp.where(low, 0, jnp.where(q == 0, GROUP, 1))
    pl.semaphore_wait(barrier, GROUP + 1 + above + below)

    own = pl.ds(pl.multiple_of(me * rows, rows), rows)
    passed = pl.ds(pl.multiple_of(cross * rows, rows), rows)

    def move(which, kind, t):
        source, full = ((a_ref, a_full), (g_ref, g_full))[which]
        if kind == 2:
            src = full.at[t, passed, :]
            dst = full.at[t, passed, :]
        else:
            src = source.at[t]
            dst = full.at[t, own, :]
        return pltpu.make_async_remote_copy(
            src_ref=src,
            dst_ref=dst,
            send_sem=send_sem.at[which, kind, t],
            recv_sem=recv_sem.at[which, kind, t],
            device_id={"col": cross if kind == 1 else sib},
            device_id_type=MESH,
        )

    def kept(which):
        source, full = ((a_ref, a_full), (g_ref, g_full))[which]
        return pltpu.make_async_copy(source, full.at[:, own, :], local_sem.at[which])

    for t in range(steps):
        move(0, 1, t).start()
    for t in range(steps):
        move(0, 0, t).start()
    kept(0).start()

    for n in range(3):
        fetch(n).wait()

    hi, lo = halves(dyn_ref[...])
    dyn_hl[0] = hi
    dyn_hl[1] = lo
    rest = jnp.zeros((PAD - series, dim), jnp.float32)

    def padded(x):
        return jnp.concatenate([x, rest], axis=0)

    def pass_on(which, t):
        move(which, 1, t).wait_recv()
        move(which, 2, t).start()

    def keep_pre(pre, t, p):
        hi, lo = halves(p)
        pre[t, 0:dim] = hi
        pre[t, dim : 2 * dim] = lo

    kept(0).wait()
    ahead = 2
    for t in range(ahead):
        pass_on(0, t)

    def arrived(which, t):
        move(which, 0, t).wait_recv()
        move(which, 2, t).wait_recv()

    arrived(0, 0)
    a_pre[0, 0:dim] = a_full[0]
    a_pre[0, dim : 2 * dim] = jnp.zeros((dim, dim), jnp.bfloat16)
    v0 = padded(drive_ref[0])
    vst[0] = v0
    a_pre[0, 2 * dim : 2 * dim + 2 * PAD] = stacked(v0)

    def forward_step(t, carry):
        @pl.when(t + ahead - 1 < steps)
        def _():
            pass_on(0, t + ahead - 1)

        arrived(0, t)
        r = dot(a_pre[t - 1], a_full[t])
        v = folded(r[2 * dim :]) + padded(drive_ref[t])
        keep_pre(a_pre, t, r[0:dim] + r[dim : 2 * dim])
        vst[t] = v
        a_pre[t, 2 * dim : 2 * dim + 2 * PAD] = stacked(v)
        return carry

    lax.fori_loop(1, steps, forward_step, 0)

    half_steps = steps // 2
    laps = [(steps - 1 - n, half_steps - 1 - n) for n in range(half_steps)]
    for pair in laps:
        for t in pair:
            move(1, 1, t).start()
    for pair in laps:
        for t in pair:
            move(1, 0, t).start()
    kept(1).start()

    half = lax.rem(me, 2)
    mine = pl.ds(pl.multiple_of(half * dim, dim), dim)

    def group_copy(way, kind, slot, d):
        pre, got, out, means = ((a_pre, a_got, v_out, v_got), (g_pre, g_got, b_out, b_got))[way]
        block = steps - 1 if way == 0 else steps
        if kind == 0:
            src, dst = pre.at[block, mine, :], got.at[slot, mine, :]
        elif kind == 1:
            src, dst = out, means.at[slot]
        else:
            src, dst = got.at[slot, mine, :], got.at[slot, mine, :]
        to = {"col": sib} if kind == 2 else {"tm": place + d if way == 0 else place - d}
        return pltpu.make_async_remote_copy(
            src_ref=src,
            dst_ref=dst,
            send_sem=group_send.at[way, kind, slot if kind == 2 else d - 1],
            recv_sem=group_recv.at[way, kind, slot],
            device_id=to,
            device_id_type=MESH,
        )

    def each_target(way, body):
        for d in reversed(range(1, GROUP)):
            pl.when(q + d <= GROUP - 1 if way == 0 else q >= d)(functools.partial(body, d))

    def spread(way, kind):
        slot = q if way == 0 else q - 1
        each_target(way, lambda d: group_copy(way, kind, slot, d).start())

    def each_source(way, body):
        for s in range(GROUP - 1) if way == 0 else reversed(range(GROUP - 1)):
            pl.when(q > s if way == 0 else q <= s)(functools.partial(body, s))

    def each_operator(way, body):
        for s in range(GROUP - 1) if way == 0 else reversed(range(GROUP - 1)):
            needed = q > s if way == 0 else q <= s
            if way == 0 and s == 0:
                needed = jnp.logical_and(needed, jnp.logical_not(low))
            if way == 1 and s == GROUP - 2:
                needed = jnp.logical_and(needed, jnp.logical_not(high))
            pl.when(needed)(functools.partial(body, s))

    def share(way):
        def one(s):
            group_copy(way, 0, s, 1).wait_recv()
            group_copy(way, 2, s, 1).start()

        each_operator(way, one)

    def applied(state, pre, block):
        r = dot(state, pre[block, 0:dim]) + dot(state, pre[block, dim : 2 * dim])
        return folded(r)

    @pl.when(low)
    def _():
        x_in[...] = padded(init_ref[...])

    @pl.when(first)
    def _():
        v_out[...] = applied(stacked(x_in[...]), a_pre, steps - 1) + vst[steps - 1]

    @pl.when(jnp.logical_not(first))
    def _():
        v_out[...] = vst[steps - 1]
        spread(0, 0)

    spread(0, 1)

    end = steps - 1

    def rows_of(t):
        return pl.ds(pl.multiple_of(t * PAD, PAD), PAD)

    def gains():
        def pass_pair(n):
            for t in laps[n]:
                pass_on(1, t)

        pass_pair(0)
        pass_pair(1)
        kept(1).wait()
        for n, pair in enumerate(laps):
            if 1 <= n < half_steps - 1:
                pass_pair(n + 1)
            for t in pair:
                arrived(1, t)
                if n == 0:
                    g_pre[t, 0:dim] = g_full[t]
                    g_pre[t, dim : 2 * dim] = jnp.zeros((dim, dim), jnp.bfloat16)
                else:
                    r = dot(g_pre[t + 1], g_full[t])
                    keep_pre(g_pre, t, r[0:dim] + r[dim : 2 * dim])

        @pl.when(jnp.logical_not(last))
        def _():
            r = dot(g_pre[half_steps], g_pre[0, 0:dim])
            more = dot(g_pre[half_steps, 0:dim], g_pre[0, dim : 2 * dim])
            keep_pre(g_pre, steps, r[0:dim] + r[dim : 2 * dim] + more)
            spread(1, 0)

    pl.when(low)(functools.partial(share, 0))

    @pl.when(jnp.logical_not(low))
    def _():
        gains()
        share(0)

    def chain(way, d):
        src, dst = ((x_out, x_in), (s_out, s_in))[way]
        return pltpu.make_async_remote_copy(
            src_ref=src,
            dst_ref=dst,
            send_sem=chain_send.at[way, d - 1],
            recv_sem=chain_recv.at[way],
            device_id={"tm": place + d if way == 0 else place - d},
            device_id_type=MESH,
        )

    @pl.when(jnp.logical_not(low))
    def _():
        chain(0, 1).wait_recv()

    def take(s):
        group_copy(0, 1, s, 1).wait_recv()

        def product():
            group_copy(0, 2, s, 1).wait_recv()
            x_in[...] = applied(stacked(x_in[...]), a_got, s) + v_got[s]

        if s == 0:
            pl.when(jnp.logical_not(low))(product)

            @pl.when(low)
            def _():
                x_in[...] = v_got[s]
        else:
            product()

    each_source(0, take)
    x = stacked(x_in[...])

    def filtered_at(t):
        f = applied(x, a_pre, t) + vst[t]
        fst[t * PAD : (t + 1) * PAD] = f
        filt_ref[t] = f[0:series]
        return f

    x_out[...] = filtered_at(end)
    gives = jnp.logical_and(q == GROUP - 1, jnp.logical_not(high))

    @pl.when(gives)
    def _():
        for d in reversed(range(1, GROUP + 1)):
            chain(0, d).start()

    for t in range(end):
        filtered_at(t)

    pl.when(low)(gains)

    f_all = stacked(fst[...])
    pst[...] = folded(dot(f_all, dyn_hl[0]) + dot(f_all, dyn_hl[1]))

    def mean_step(state, t):
        moved = -pst[rows_of(t)] if state is None else state - pst[rows_of(t)]
        now = folded(dot(stacked(moved), g_full[t]))
        if t == end:
            now = jnp.where(last, jnp.zeros_like(now), now)
        now = now + fst[rows_of(t)]
        lst[t] = now
        return now

    upper = lower = None
    for t_up, t_low in laps:
        upper = mean_step(upper, t_up)
        lower = mean_step(lower, t_low)
    b_out[...] = applied(stacked(upper), g_pre, 0) + lower
    spread(1, 1)
    share(1)

    @pl.when(high)
    def _():
        s_in[...] = jnp.zeros((PAD, dim), jnp.float32)

    @pl.when(jnp.logical_not(high))
    def _():
        chain(1, 1).wait_recv()

    def take_back(s):
        group_copy(1, 1, s, 1).wait_recv()

        def product():
            group_copy(1, 2, s, 1).wait_recv()
            s_in[...] = applied(stacked(s_in[...]), g_got, s) + b_got[s]

        if s == GROUP - 2:
            pl.when(jnp.logical_not(high))(product)

            @pl.when(high)
            def _():
                s_in[...] = b_got[s]
        else:
            product()

    each_source(1, take_back)

    returns = jnp.logical_and(q == 0, jnp.logical_not(low))

    @pl.when(last)
    def _():
        smooth_ref[0] = b_out[0:series]
        for t in range(half_steps, steps):
            smooth_ref[t] = lst[t][0:series]

    @pl.when(jnp.logical_not(last))
    def _():
        s = stacked(s_in[...])
        now = applied(s, g_pre, steps) + b_out[...]
        s_out[...] = now
        smooth_ref[0] = now[0:series]

        @pl.when(returns)
        def _():
            for d in reversed(range(1, GROUP + 1)):
                chain(1, d).start()

        for t in range(half_steps, steps):
            now = applied(s, g_pre, t) + lst[t]
            smooth_ref[t] = now[0:series]
            if t == half_steps:
                lst[t] = now

    middle = stacked(lst[half_steps])
    for t in range(1, half_steps):
        smooth_ref[t] = (applied(middle, g_pre, t) + lst[t])[0:series]

    def sent(t, carry):
        for which in range(2):
            for kind in range(3):
                move(which, kind, t).wait_send()
        return carry

    lax.fori_loop(0, steps, sent, 0)

    for way, final in ((0, first), (1, last)):

        def done(kind, d):
            group_copy(way, kind, 0, d).wait_send()

        @pl.when(jnp.logical_not(final))
        def _():
            each_target(way, functools.partial(done, 0))

        each_target(way, functools.partial(done, 1))
        each_operator(way, lambda s: group_copy(way, 2, s, 1).wait_send())

    for way, sender in ((0, gives), (1, returns)):
        @pl.when(sender)
        def _():
            for d in range(1, GROUP + 1):
                chain(way, d).wait_send()


def local(blocks, transition, drive, smoother_gain, dynamics, initial_mean):
    steps, rows, dim = transition.shape
    series = initial_mean.shape[0]
    vmem = pl.BlockSpec(memory_space=pltpu.VMEM)
    hbm = pl.BlockSpec(memory_space=pltpu.HBM)
    full = pltpu.VMEM((steps, dim, dim), jnp.bfloat16)
    a_pre = pltpu.VMEM((steps, 2 * dim + 2 * PAD, dim), jnp.bfloat16)
    g_pre = pltpu.VMEM((steps + 1, 2 * dim, dim), jnp.bfloat16)
    got = pltpu.VMEM((GROUP - 1, 2 * dim, dim), jnp.bfloat16)
    group = pltpu.VMEM((GROUP - 1, PAD, dim), jnp.float32)
    means = pltpu.VMEM((steps, PAD, dim), jnp.float32)
    flat = pltpu.VMEM((steps * PAD, dim), jnp.float32)
    one = pltpu.VMEM((PAD, dim), jnp.float32)
    out = jax.ShapeDtypeStruct(drive.shape, jnp.float32)
    return pl.pallas_call(
        functools.partial(kernel, blocks, steps, rows, series),
        out_shape=(out, out),
        in_specs=[hbm] * 5,
        out_specs=(vmem, vmem),
        scratch_shapes=[
            pltpu.VMEM(drive.shape, drive.dtype),
            pltpu.VMEM(dynamics.shape, dynamics.dtype),
            pltpu.VMEM(initial_mean.shape, initial_mean.dtype),
            full, full, a_pre, g_pre, got, got, group, group, one, one,
            means, flat, means, flat,
            pltpu.VMEM((2, dim, dim), jnp.bfloat16),
            one, one, one, one,
            pltpu.SemaphoreType.DMA((5,)),
            pltpu.SemaphoreType.DMA((2, 3, steps)),
            pltpu.SemaphoreType.DMA((2, 3, steps)),
            pltpu.SemaphoreType.DMA((2, 3, GROUP - 1)),
            pltpu.SemaphoreType.DMA((2, 3, GROUP - 1)),
            pltpu.SemaphoreType.DMA((2, GROUP)),
            pltpu.SemaphoreType.DMA((2,)),
        ],
        compiler_params=pltpu.CompilerParams(
            collective_id=0, has_side_effects=True, vmem_limit_bytes=60 * 1024 * 1024
        ),
    )(transition, smoother_gain, drive, dynamics, initial_mean)


def solution(mesh):
    placed = (P("tm", "col", None), P("tm", "col", None), P("tm", "col", None), P(), P("col", None))
    return jax.shard_map(
        functools.partial(local, mesh.shape["tm"]),
        mesh=mesh,
        in_specs=placed,
        out_specs=(P("tm", "col", None), P("tm", "col", None)),
        check_vma=False,
    )
```

```python
import functools

import jax
import jax.numpy as jnp
from jax import lax
from jax.experimental import pallas as pl
from jax.experimental.pallas import tpu as pltpu
from jax.sharding import PartitionSpec as P

MESH = pl.DeviceIdType.MESH
PAD = 8
GROUP = 4


def dot(left, right):
    return jnp.dot(left, right, preferred_element_type=jnp.float32)


def halves(x):
    hi = x.astype(jnp.bfloat16)
    lo = (x - hi.astype(jnp.float32)).astype(jnp.bfloat16)
    return hi, lo


def stacked(x):
    hi = x.astype(jnp.bfloat16).astype(jnp.float32)
    return jnp.concatenate([hi, x - hi], axis=0).astype(jnp.bfloat16)


def folded(r):
    rows = r.shape[0] // 2
    return r[:rows] + r[rows:]


def kernel(
    blocks, steps, rows, series,
    a_ref, g_ref, drive_hbm, dyn_hbm, init_hbm, filt_ref, smooth_ref,
    drive_ref, dyn_ref, init_ref,
    a_full, g_full, a_pre, g_pre, a_got, g_got, v_got, b_got, v_out, b_out, e_pre, e_vec,
    vst, fst, lst, pst, dyn_hl, x_out, x_in, s_out, s_in,
    local_sem, send_sem, recv_sem, group_send, group_recv, chain_send, chain_recv,
):
    dim = dyn_ref.shape[0]

    def fetch(n):
        src, dst = ((drive_hbm, drive_ref), (dyn_hbm, dyn_ref), (init_hbm, init_ref))[n]
        return pltpu.make_async_copy(src, dst, local_sem.at[2 + n])

    for n in range(3):
        fetch(n).start()
    place = lax.axis_index("tm")
    me = lax.axis_index("col")
    sib = me + 1 - 2 * lax.rem(me, 2)
    cross = lax.rem(me + 2, 4)
    q = lax.rem(place, GROUP)
    begin = place - q
    first = place == 0
    last = place == blocks - 1
    low = begin == 0
    high = begin == blocks - GROUP

    barrier = pltpu.get_barrier_semaphore()

    def greet(other):
        pl.semaphore_signal(barrier, inc=1, device_id=other, device_id_type=MESH)

    greet({"col": sib})
    greet({"col": cross})
    for d in range(1, GROUP):
        greet({"tm": begin + lax.rem(q + d, GROUP)})

    @pl.when(jnp.logical_not(high))
    def _():
        greet({"tm": begin + GROUP})

        @pl.when(q == GROUP - 1)
        def _():
            for d in range(1, GROUP):
                greet({"tm": begin + GROUP + d})

    @pl.when(jnp.logical_not(low))
    def _():
        greet({"tm": begin - 1})

        @pl.when(q == 0)
        def _():
            for d in range(1, GROUP):
                greet({"tm": begin - 1 - d})

    above = jnp.where(high, 0, jnp.where(q == GROUP - 1, GROUP, 1))
    below = jnp.where(low, 0, jnp.where(q == 0, GROUP, 1))
    pl.semaphore_wait(barrier, GROUP + 1 + above + below)

    own = pl.ds(pl.multiple_of(me * rows, rows), rows)
    passed = pl.ds(pl.multiple_of(cross * rows, rows), rows)

    def move(which, kind, t):
        source, full = ((a_ref, a_full), (g_ref, g_full))[which]
        if kind == 2:
            src = full.at[t, passed, :]
            dst = full.at[t, passed, :]
        else:
            src = source.at[t]
            dst = full.at[t, own, :]
        return pltpu.make_async_remote_copy(
            src_ref=src,
            dst_ref=dst,
            send_sem=send_sem.at[which, kind, t],
            recv_sem=recv_sem.at[which, kind, t],
            device_id={"col": cross if kind == 1 else sib},
            device_id_type=MESH,
        )

    def kept(which):
        source, full = ((a_ref, a_full), (g_ref, g_full))[which]
        return pltpu.make_async_copy(source, full.at[:, own, :], local_sem.at[which])

    for t in range(steps):
        move(0, 1, t).start()
    for t in range(steps):
        move(0, 0, t).start()
    kept(0).start()
    kept(1).start()
    half_steps = steps // 2

    def lap_steps(n):
        return steps - 1 - n, half_steps - 1 - n


    for n in range(3):
        fetch(n).wait()

    hi, lo = halves(dyn_ref[...])
    dyn_hl[0] = hi
    dyn_hl[1] = lo
    rest = jnp.zeros((PAD - series, dim), jnp.float32)

    def padded(x):
        return jnp.concatenate([x, rest], axis=0)

    def pass_on(which, t):
        move(which, 1, t).wait_recv()
        move(which, 2, t).start()

    def keep_pre(pre, t, p):
        hi, lo = halves(p)
        pre[t, 0:dim] = hi
        pre[t, dim : 2 * dim] = lo

    kept(0).wait()
    ahead = 3
    for t in range(ahead):
        pass_on(0, t)

    def arrived(which, t):
        move(which, 0, t).wait_recv()
        move(which, 2, t).wait_recv()

    arrived(0, 0)
    a_pre[0, 0:dim] = a_full[0]
    a_pre[0, dim : 2 * dim] = jnp.zeros((dim, dim), jnp.bfloat16)
    v0 = padded(drive_ref[0])
    vst[0] = v0
    a_pre[0, 2 * dim : 2 * dim + 2 * PAD] = stacked(v0)

    def forward_step(t, carry):
        @pl.when(t + ahead - 1 < steps)
        def _():
            pass_on(0, t + ahead - 1)

        @pl.when(t >= steps - half_steps)
        def _():
            for g in lap_steps(t - (steps - half_steps)):
                move(1, 1, g).start()
                move(1, 0, g).start()

        arrived(0, t)
        r = dot(a_pre[t - 1], a_full[t])
        v = folded(r[2 * dim :]) + padded(drive_ref[t])
        keep_pre(a_pre, t, r[0:dim] + r[dim : 2 * dim])
        vst[t] = v
        a_pre[t, 2 * dim : 2 * dim + 2 * PAD] = stacked(v)
        return carry

    lax.fori_loop(1, steps, forward_step, 0)

    half = lax.rem(me, 2)
    mine = pl.ds(pl.multiple_of(half * dim, dim), dim)

    def group_copy(way, kind, slot, d):
        pre, got, out, means = ((a_pre, a_got, v_out, v_got), (g_pre, g_got, b_out, b_got))[way]
        block = steps - 1 if way == 0 else steps
        if kind == 0:
            src, dst = pre.at[block, mine, :], got.at[slot, mine, :]
        elif kind == 1:
            src, dst = out, means.at[slot]
        else:
            src, dst = got.at[slot, mine, :], got.at[slot, mine, :]
        to = {"col": sib} if kind == 2 else {"tm": place + d if way == 0 else place - d}
        return pltpu.make_async_remote_copy(
            src_ref=src,
            dst_ref=dst,
            send_sem=group_send.at[way, kind, slot if kind == 2 else d - 1],
            recv_sem=group_recv.at[way, kind, slot],
            device_id=to,
            device_id_type=MESH,
        )

    def each_target(way, body):
        for d in reversed(range(1, GROUP)):
            pl.when(q + d <= GROUP - 1 if way == 0 else q >= d)(functools.partial(body, d))

    def spread(way, kind):
        slot = q if way == 0 else q - 1
        each_target(way, lambda d: group_copy(way, kind, slot, d).start())

    def each_source(way, body):
        for s in range(GROUP - 1) if way == 0 else reversed(range(GROUP - 1)):
            pl.when(q > s if way == 0 else q <= s)(functools.partial(body, s))

    def each_operator(way, body):
        for s in range(GROUP - 1) if way == 0 else reversed(range(GROUP - 1)):
            needed = q > s if way == 0 else q <= s
            if way == 0 and s == 0:
                needed = jnp.logical_and(needed, jnp.logical_not(low))
            if way == 1 and s == GROUP - 2:
                needed = jnp.logical_and(needed, jnp.logical_not(high))
            pl.when(needed)(functools.partial(body, s))

    def share(way):
        def one(s):
            group_copy(way, 0, s, 1).wait_recv()
            group_copy(way, 2, s, 1).start()

        each_operator(way, one)

    def applied(state, pre, block):
        r = dot(state, pre[block, 0:dim]) + dot(state, pre[block, dim : 2 * dim])
        return folded(r)

    @pl.when(low)
    def _():
        x_in[...] = padded(init_ref[...])

    @pl.when(first)
    def _():
        v_out[...] = applied(stacked(x_in[...]), a_pre, steps - 1) + vst[steps - 1]

    @pl.when(jnp.logical_not(first))
    def _():
        v_out[...] = vst[steps - 1]
        spread(0, 0)

    spread(0, 1)

    end = steps - 1

    def rows_of(t):
        return pl.ds(pl.multiple_of(t * PAD, PAD), PAD)

    def joined(left, i, right, j):
        r = dot(left[i, 0 : 2 * dim], right[j, 0:dim])
        more = dot(left[i, 0:dim], right[j, dim : 2 * dim])
        return r[0:dim] + r[dim : 2 * dim] + more

    def gains():
        def pass_pair(n):
            for t in lap_steps(n):
                pass_on(1, t)

        pass_pair(0)
        pass_pair(1)
        kept(1).wait()
        for t in lap_steps(0):
            arrived(1, t)
            g_pre[t, 0:dim] = g_full[t]
            g_pre[t, dim : 2 * dim] = jnp.zeros((dim, dim), jnp.bfloat16)

        def lap(n, carry):
            @pl.when(n < half_steps - 1)
            def _():
                pass_pair(n + 1)

            for t in lap_steps(n):
                arrived(1, t)
                r = dot(g_pre[t + 1], g_full[t])
                keep_pre(g_pre, t, r[0:dim] + r[dim : 2 * dim])
            return carry

        lax.fori_loop(1, half_steps, lap, 0)

        @pl.when(jnp.logical_not(last))
        def _():
            keep_pre(g_pre, steps, joined(g_pre, half_steps, g_pre, 0))
            spread(1, 0)

    def chain(way, d):
        src, dst = ((x_out, x_in), (s_out, s_in))[way]
        return pltpu.make_async_remote_copy(
            src_ref=src,
            dst_ref=dst,
            send_sem=chain_send.at[way, d - 1],
            recv_sem=chain_recv.at[way],
            device_id={"tm": place + d if way == 0 else place - d},
            device_id_type=MESH,
        )

    gives = jnp.logical_and(q == GROUP - 1, jnp.logical_not(high))

    def filtering():
        share(0)

        @pl.when(jnp.logical_not(low))
        def _():
            chain(0, 1).wait_recv()

        def take(s):
            group_copy(0, 1, s, 1).wait_recv()

            def product():
                group_copy(0, 2, s, 1).wait_recv()
                x_in[...] = applied(stacked(x_in[...]), a_got, s) + v_got[s]

            if s == 0:
                pl.when(jnp.logical_not(low))(product)

                @pl.when(low)
                def _():
                    x_in[...] = v_got[s]
            else:
                product()

        each_source(0, take)
        x = stacked(x_in[...])

        def filtered_at(t):
            f = applied(x, a_pre, t) + vst[t]
            fst[t * PAD : (t + 1) * PAD] = f
            filt_ref[t] = f[0:series]
            return f

        x_out[...] = filtered_at(end)

        @pl.when(gives)
        def _():
            for d in reversed(range(1, GROUP + 1)):
                chain(0, d).start()

        for t in range(end):
            filtered_at(t)

    def phase(n, carry):
        pl.when(low == (n == 1))(gains)
        pl.when(n == 0)(filtering)
        return carry

    lax.fori_loop(0, 2, phase, 0)

    f_all = stacked(fst[...])
    pst[...] = folded(dot(f_all, dyn_hl[0]) + dot(f_all, dyn_hl[1]))

    def mean_step(state, t):
        moved = -pst[rows_of(t)] if state is None else state - pst[rows_of(t)]
        now = folded(dot(stacked(moved), g_full[t]))
        if t == end:
            now = jnp.where(last, jnp.zeros_like(now), now)
        now = now + fst[rows_of(t)]
        lst[t] = now
        return now

    upper = lower = None
    for t_up, t_low in map(lap_steps, range(half_steps)):
        upper = mean_step(upper, t_up)
        lower = mean_step(lower, t_low)
    b_out[...] = applied(stacked(upper), g_pre, 0) + lower
    spread(1, 1)
    share(1)

    @pl.when(q == GROUP - 1)
    def _():
        e_vec[...] = jnp.zeros((PAD, dim), jnp.float32)

    def take_back(s):
        group_copy(1, 1, s, 1).wait_recv()
        if s == GROUP - 2:
            e_vec[...] = b_got[s]

            @pl.when(jnp.logical_not(high))
            def _():
                group_copy(1, 2, s, 1).wait_recv()
                e_pre[0] = g_got[s]
        else:
            group_copy(1, 2, s, 1).wait_recv()
            e_vec[...] = applied(stacked(e_vec[...]), g_got, s) + b_got[s]

            @pl.when(jnp.logical_not(high))
            def _():
                keep_pre(e_pre, 0, joined(e_pre, 0, g_got, s))

    each_source(1, take_back)

    @pl.when(high)
    def _():
        s_in[...] = e_vec[...]

    @pl.when(jnp.logical_not(high))
    def _():
        chain(1, 1).wait_recv()

        @pl.when(q < GROUP - 1)
        def _():
            s_in[...] = applied(stacked(s_in[...]), e_pre, 0) + e_vec[...]

    returns = jnp.logical_and(q == 0, jnp.logical_not(low))

    @pl.when(last)
    def _():
        smooth_ref[0] = b_out[0:series]
        for t in range(half_steps, steps):
            smooth_ref[t] = lst[t][0:series]

    @pl.when(jnp.logical_not(last))
    def _():
        s = stacked(s_in[...])
        now = applied(s, g_pre, steps) + b_out[...]
        s_out[...] = now
        smooth_ref[0] = now[0:series]

        @pl.when(returns)
        def _():
            for d in reversed(range(1, GROUP + 1)):
                chain(1, d).start()

        for t in range(half_steps, steps):
            now = applied(s, g_pre, t) + lst[t]
            smooth_ref[t] = now[0:series]
            if t == half_steps:
                lst[t] = now

    middle = stacked(lst[half_steps])
    for t in range(1, half_steps):
        smooth_ref[t] = (applied(middle, g_pre, t) + lst[t])[0:series]

    def sent(t, carry):
        for which in range(2):
            for kind in range(3):
                move(which, kind, t).wait_send()
        return carry

    lax.fori_loop(0, steps, sent, 0)

    for way, final in ((0, first), (1, last)):

        def done(kind, d):
            group_copy(way, kind, 0, d).wait_send()

        @pl.when(jnp.logical_not(final))
        def _():
            each_target(way, functools.partial(done, 0))

        each_target(way, functools.partial(done, 1))
        each_operator(way, lambda s: group_copy(way, 2, s, 1).wait_send())

    for way, sender in ((0, gives), (1, returns)):
        @pl.when(sender)
        def _():
            for d in range(1, GROUP + 1):
                chain(way, d).wait_send()


def local(blocks, transition, drive, smoother_gain, dynamics, initial_mean):
    steps, rows, dim = transition.shape
    series = initial_mean.shape[0]
    vmem = pl.BlockSpec(memory_space=pltpu.VMEM)
    hbm = pl.BlockSpec(memory_space=pltpu.HBM)
    full = pltpu.VMEM((steps, dim, dim), jnp.bfloat16)
    a_pre = pltpu.VMEM((steps, 2 * dim + 2 * PAD, dim), jnp.bfloat16)
    g_pre = pltpu.VMEM((steps + 1, 2 * dim, dim), jnp.bfloat16)
    got = pltpu.VMEM((GROUP - 1, 2 * dim, dim), jnp.bfloat16)
    group = pltpu.VMEM((GROUP - 1, PAD, dim), jnp.float32)
    means = pltpu.VMEM((steps, PAD, dim), jnp.float32)
    flat = pltpu.VMEM((steps * PAD, dim), jnp.float32)
    one = pltpu.VMEM((PAD, dim), jnp.float32)
    out = jax.ShapeDtypeStruct(drive.shape, jnp.float32)
    return pl.pallas_call(
        functools.partial(kernel, blocks, steps, rows, series),
        out_shape=(out, out),
        in_specs=[hbm] * 5,
        out_specs=(vmem, vmem),
        scratch_shapes=[
            pltpu.VMEM(drive.shape, drive.dtype),
            pltpu.VMEM(dynamics.shape, dynamics.dtype),
            pltpu.VMEM(initial_mean.shape, initial_mean.dtype),
            full, full, a_pre, g_pre, got, got, group, group, one, one,
            pltpu.VMEM((1, 2 * dim, dim), jnp.bfloat16), one,
            means, flat, means, flat,
            pltpu.VMEM((2, dim, dim), jnp.bfloat16),
            one, one, one, one,
            pltpu.SemaphoreType.DMA((5,)),
            pltpu.SemaphoreType.DMA((2, 3, steps)),
            pltpu.SemaphoreType.DMA((2, 3, steps)),
            pltpu.SemaphoreType.DMA((2, 3, GROUP - 1)),
            pltpu.SemaphoreType.DMA((2, 3, GROUP - 1)),
            pltpu.SemaphoreType.DMA((2, GROUP)),
            pltpu.SemaphoreType.DMA((2,)),
        ],
        compiler_params=pltpu.CompilerParams(
            collective_id=0, has_side_effects=True, vmem_limit_bytes=60 * 1024 * 1024
        ),
    )(transition, smoother_gain, drive, dynamics, initial_mean)


def solution(mesh):
    placed = (P("tm", "col", None), P("tm", "col", None), P("tm", "col", None), P(), P("col", None))
    return jax.shard_map(
        functools.partial(local, mesh.shape["tm"]),
        mesh=mesh,
        in_specs=placed,
        out_specs=(P("tm", "col", None), P("tm", "col", None)),
        check_vma=False,
    )
```

```python
import functools

import jax
import jax.numpy as jnp
from jax import lax
from jax.experimental import pallas as pl
from jax.experimental.pallas import tpu as pltpu
from jax.sharding import PartitionSpec as P

MESH = pl.DeviceIdType.MESH
PAD = 8
GROUP = 4


def dot(left, right):
    return jnp.dot(left, right, preferred_element_type=jnp.float32)


def halves(x):
    hi = x.astype(jnp.bfloat16)
    lo = (x - hi.astype(jnp.float32)).astype(jnp.bfloat16)
    return hi, lo


def stacked(x):
    hi = x.astype(jnp.bfloat16).astype(jnp.float32)
    return jnp.concatenate([hi, x - hi], axis=0).astype(jnp.bfloat16)


def folded(r):
    rows = r.shape[0] // 2
    return r[:rows] + r[rows:]


def kernel(
    blocks, steps, rows, series,
    a_ref, g_ref, drive_hbm, dyn_hbm, init_hbm, filt_ref, smooth_ref,
    drive_ref, dyn_ref, init_ref,
    a_full, g_full, a_pre, g_pre, a_got, g_got, v_got, b_got, v_out, b_out, e_pre, e_vec, d_pre, d_vec,
    vst, fst, lst, pst, dyn_hl, x_out, x_in, s_out, s_in,
    local_sem, send_sem, recv_sem, group_send, group_recv, chain_send, chain_recv,
):
    dim = dyn_ref.shape[0]

    def fetch(n):
        src, dst = ((drive_hbm, drive_ref), (dyn_hbm, dyn_ref), (init_hbm, init_ref))[n]
        return pltpu.make_async_copy(src, dst, local_sem.at[2 + n])

    for n in range(3):
        fetch(n).start()
    place = lax.axis_index("tm")
    me = lax.axis_index("col")
    sib = me + 1 - 2 * lax.rem(me, 2)
    cross = lax.rem(me + 2, 4)
    q = lax.rem(place, GROUP)
    begin = place - q
    first = place == 0
    last = place == blocks - 1
    low = begin == 0
    high = begin == blocks - GROUP

    barrier = pltpu.get_barrier_semaphore()

    def greet(other):
        pl.semaphore_signal(barrier, inc=1, device_id=other, device_id_type=MESH)

    greet({"col": sib})
    greet({"col": cross})
    for d in range(1, GROUP):
        greet({"tm": begin + lax.rem(q + d, GROUP)})

    @pl.when(jnp.logical_not(high))
    def _():
        greet({"tm": begin + GROUP})

        @pl.when(q == GROUP - 1)
        def _():
            for d in range(1, GROUP):
                greet({"tm": begin + GROUP + d})

    @pl.when(jnp.logical_not(low))
    def _():
        greet({"tm": begin - 1})

        @pl.when(q == 0)
        def _():
            for d in range(1, GROUP):
                greet({"tm": begin - 1 - d})

    above = jnp.where(high, 0, jnp.where(q == GROUP - 1, GROUP, 1))
    below = jnp.where(low, 0, jnp.where(q == 0, GROUP, 1))
    pl.semaphore_wait(barrier, GROUP + 1 + above + below)

    own = pl.ds(pl.multiple_of(me * rows, rows), rows)
    passed = pl.ds(pl.multiple_of(cross * rows, rows), rows)

    def move(which, kind, t):
        source, full = ((a_ref, a_full), (g_ref, g_full))[which]
        if kind == 2:
            src = full.at[t, passed, :]
            dst = full.at[t, passed, :]
        else:
            src = source.at[t]
            dst = full.at[t, own, :]
        return pltpu.make_async_remote_copy(
            src_ref=src,
            dst_ref=dst,
            send_sem=send_sem.at[which, kind, t],
            recv_sem=recv_sem.at[which, kind, t],
            device_id={"col": cross if kind == 1 else sib},
            device_id_type=MESH,
        )

    def kept(which):
        source, full = ((a_ref, a_full), (g_ref, g_full))[which]
        return pltpu.make_async_copy(source, full.at[:, own, :], local_sem.at[which])

    for t in range(steps):
        move(0, 1, t).start()
    for t in range(steps):
        move(0, 0, t).start()
    kept(0).start()
    kept(1).start()
    half_steps = steps // 2

    def lap_steps(n):
        return steps - 1 - n, half_steps - 1 - n


    for n in range(3):
        fetch(n).wait()

    hi, lo = halves(dyn_ref[...])
    dyn_hl[0] = hi
    dyn_hl[1] = lo
    rest = jnp.zeros((PAD - series, dim), jnp.float32)

    def padded(x):
        return jnp.concatenate([x, rest], axis=0)

    def pass_on(which, t):
        move(which, 1, t).wait_recv()
        move(which, 2, t).start()

    def keep_pre(pre, t, p):
        hi, lo = halves(p)
        pre[t, 0:dim] = hi
        pre[t, dim : 2 * dim] = lo

    kept(0).wait()
    ahead = 3
    for t in range(ahead):
        pass_on(0, t)

    def arrived(which, t):
        move(which, 0, t).wait_recv()
        move(which, 2, t).wait_recv()

    arrived(0, 0)
    a_pre[0, 0:dim] = a_full[0]
    a_pre[0, dim : 2 * dim] = jnp.zeros((dim, dim), jnp.bfloat16)
    v0 = padded(drive_ref[0])
    vst[0] = v0
    a_pre[0, 2 * dim : 2 * dim + 2 * PAD] = stacked(v0)

    def forward_step(t, carry):
        @pl.when(t + ahead - 1 < steps)
        def _():
            pass_on(0, t + ahead - 1)

        @pl.when(t >= steps - half_steps)
        def _():
            for g in lap_steps(t - (steps - half_steps)):
                move(1, 1, g).start()
                move(1, 0, g).start()

        arrived(0, t)
        r = dot(a_pre[t - 1], a_full[t])
        v = folded(r[2 * dim :]) + padded(drive_ref[t])
        keep_pre(a_pre, t, r[0:dim] + r[dim : 2 * dim])
        vst[t] = v
        a_pre[t, 2 * dim : 2 * dim + 2 * PAD] = stacked(v)
        return carry

    lax.fori_loop(1, steps, forward_step, 0)

    half = lax.rem(me, 2)
    mine = pl.ds(pl.multiple_of(half * dim, dim), dim)

    def group_copy(way, kind, slot, d):
        pre, got, out, means = ((a_pre, a_got, v_out, v_got), (g_pre, g_got, b_out, b_got))[way]
        block = steps - 1 if way == 0 else steps
        if kind == 0:
            src, dst = pre.at[block, mine, :], got.at[slot, mine, :]
        elif kind == 1:
            src, dst = out, means.at[slot]
        else:
            src, dst = got.at[slot, mine, :], got.at[slot, mine, :]
        to = {"col": sib} if kind == 2 else {"tm": place + d if way == 0 else place - d}
        return pltpu.make_async_remote_copy(
            src_ref=src,
            dst_ref=dst,
            send_sem=group_send.at[way, kind, slot if kind == 2 else d - 1],
            recv_sem=group_recv.at[way, kind, slot],
            device_id=to,
            device_id_type=MESH,
        )

    def each_target(way, body):
        for d in reversed(range(1, GROUP)):
            pl.when(q + d <= GROUP - 1 if way == 0 else q >= d)(functools.partial(body, d))

    def spread(way, kind):
        slot = q if way == 0 else q - 1
        each_target(way, lambda d: group_copy(way, kind, slot, d).start())

    def each_source(way, body):
        for s in range(GROUP - 1) if way == 0 else reversed(range(GROUP - 1)):
            pl.when(q > s if way == 0 else q <= s)(functools.partial(body, s))

    def each_operator(way, body):
        for s in range(GROUP - 1) if way == 0 else reversed(range(GROUP - 1)):
            needed = q > s if way == 0 else q <= s
            if way == 0 and s == 0:
                needed = jnp.logical_and(needed, jnp.logical_not(low))
            if way == 1 and s == GROUP - 2:
                needed = jnp.logical_and(needed, jnp.logical_not(high))
            pl.when(needed)(functools.partial(body, s))

    def share(way):
        def one(s):
            group_copy(way, 0, s, 1).wait_recv()
            group_copy(way, 2, s, 1).start()

        each_operator(way, one)

    def applied(state, pre, block):
        r = dot(state, pre[block, 0:dim]) + dot(state, pre[block, dim : 2 * dim])
        return folded(r)

    @pl.when(low)
    def _():
        x_in[...] = padded(init_ref[...])

    @pl.when(first)
    def _():
        v_out[...] = applied(stacked(x_in[...]), a_pre, steps - 1) + vst[steps - 1]

    @pl.when(jnp.logical_not(first))
    def _():
        v_out[...] = vst[steps - 1]
        spread(0, 0)

    spread(0, 1)

    end = steps - 1

    def rows_of(t):
        return pl.ds(pl.multiple_of(t * PAD, PAD), PAD)

    def joined(left, i, right, j):
        r = dot(left[i, 0 : 2 * dim], right[j, 0:dim])
        more = dot(left[i, 0:dim], right[j, dim : 2 * dim])
        return r[0:dim] + r[dim : 2 * dim] + more

    def gains():
        def pass_pair(n):
            for t in lap_steps(n):
                pass_on(1, t)

        pass_pair(0)
        pass_pair(1)
        kept(1).wait()
        for t in lap_steps(0):
            arrived(1, t)
            g_pre[t, 0:dim] = g_full[t]
            g_pre[t, dim : 2 * dim] = jnp.zeros((dim, dim), jnp.bfloat16)

        def lap(n, carry):
            @pl.when(n < half_steps - 1)
            def _():
                pass_pair(n + 1)

            for t in lap_steps(n):
                arrived(1, t)
                r = dot(g_pre[t + 1], g_full[t])
                keep_pre(g_pre, t, r[0:dim] + r[dim : 2 * dim])
            return carry

        lax.fori_loop(1, half_steps, lap, 0)

        @pl.when(jnp.logical_not(last))
        def _():
            keep_pre(g_pre, steps, joined(g_pre, half_steps, g_pre, 0))
            spread(1, 0)

    def chain(way, d):
        src, dst = ((x_out, x_in), (s_out, s_in))[way]
        return pltpu.make_async_remote_copy(
            src_ref=src,
            dst_ref=dst,
            send_sem=chain_send.at[way, d - 1],
            recv_sem=chain_recv.at[way],
            device_id={"tm": place + d if way == 0 else place - d},
            device_id_type=MESH,
        )

    gives = jnp.logical_and(q == GROUP - 1, jnp.logical_not(high))

    def filtering():
        share(0)

        def take(s):
            group_copy(0, 1, s, 1).wait_recv()
            if s == 0:
                d_vec[...] = v_got[s]

                @pl.when(jnp.logical_not(low))
                def _():
                    group_copy(0, 2, s, 1).wait_recv()
                    d_pre[0] = a_got[s]
            else:
                group_copy(0, 2, s, 1).wait_recv()
                d_vec[...] = applied(stacked(d_vec[...]), a_got, s) + v_got[s]

                @pl.when(jnp.logical_not(low))
                def _():
                    keep_pre(d_pre, 0, joined(d_pre, 0, a_got, s))

        each_source(0, take)

        @pl.when(jnp.logical_and(low, q > 0))
        def _():
            x_in[...] = d_vec[...]

        @pl.when(jnp.logical_not(low))
        def _():
            chain(0, 1).wait_recv()

            @pl.when(q > 0)
            def _():
                x_in[...] = applied(stacked(x_in[...]), d_pre, 0) + d_vec[...]

        x = stacked(x_in[...])

        def filtered_at(t):
            f = applied(x, a_pre, t) + vst[t]
            fst[t * PAD : (t + 1) * PAD] = f
            filt_ref[t] = f[0:series]
            return f

        x_out[...] = filtered_at(end)

        @pl.when(gives)
        def _():
            for d in reversed(range(1, GROUP + 1)):
                chain(0, d).start()

        for t in range(end):
            filtered_at(t)

    hurry = jnp.logical_and(low, q == GROUP - 1)

    def phase(n, carry):
        pl.when(hurry == (n == 1))(gains)
        pl.when(n == 0)(filtering)
        return carry

    lax.fori_loop(0, 2, phase, 0)

    f_all = stacked(fst[...])
    pst[...] = folded(dot(f_all, dyn_hl[0]) + dot(f_all, dyn_hl[1]))

    def mean_step(state, t):
        moved = -pst[rows_of(t)] if state is None else state - pst[rows_of(t)]
        now = folded(dot(stacked(moved), g_full[t]))
        if t == end:
            now = jnp.where(last, jnp.zeros_like(now), now)
        now = now + fst[rows_of(t)]
        lst[t] = now
        return now

    upper = lower = None
    for t_up, t_low in map(lap_steps, range(half_steps)):
        upper = mean_step(upper, t_up)
        lower = mean_step(lower, t_low)
    b_out[...] = applied(stacked(upper), g_pre, 0) + lower
    spread(1, 1)
    share(1)

    @pl.when(q == GROUP - 1)
    def _():
        e_vec[...] = jnp.zeros((PAD, dim), jnp.float32)

    def take_back(s):
        group_copy(1, 1, s, 1).wait_recv()
        if s == GROUP - 2:
            e_vec[...] = b_got[s]

            @pl.when(jnp.logical_not(high))
            def _():
                group_copy(1, 2, s, 1).wait_recv()
                e_pre[0] = g_got[s]
        else:
            group_copy(1, 2, s, 1).wait_recv()
            e_vec[...] = applied(stacked(e_vec[...]), g_got, s) + b_got[s]

            @pl.when(jnp.logical_not(high))
            def _():
                keep_pre(e_pre, 0, joined(e_pre, 0, g_got, s))

    each_source(1, take_back)

    @pl.when(high)
    def _():
        s_in[...] = e_vec[...]

    @pl.when(jnp.logical_not(high))
    def _():
        chain(1, 1).wait_recv()

        @pl.when(q < GROUP - 1)
        def _():
            s_in[...] = applied(stacked(s_in[...]), e_pre, 0) + e_vec[...]

    returns = jnp.logical_and(q == 0, jnp.logical_not(low))

    @pl.when(last)
    def _():
        smooth_ref[0] = b_out[0:series]
        for t in range(half_steps, steps):
            smooth_ref[t] = lst[t][0:series]

    @pl.when(jnp.logical_not(last))
    def _():
        s = stacked(s_in[...])
        now = applied(s, g_pre, steps) + b_out[...]
        s_out[...] = now
        smooth_ref[0] = now[0:series]

        @pl.when(returns)
        def _():
            for d in reversed(range(1, GROUP + 1)):
                chain(1, d).start()

        for t in range(half_steps, steps):
            now = applied(s, g_pre, t) + lst[t]
            smooth_ref[t] = now[0:series]
            if t == half_steps:
                lst[t] = now

    middle = stacked(lst[half_steps])
    for t in range(1, half_steps):
        smooth_ref[t] = (applied(middle, g_pre, t) + lst[t])[0:series]

    def sent(t, carry):
        for which in range(2):
            for kind in range(3):
                move(which, kind, t).wait_send()
        return carry

    lax.fori_loop(0, steps, sent, 0)

    for way, final in ((0, first), (1, last)):

        def done(kind, d):
            group_copy(way, kind, 0, d).wait_send()

        @pl.when(jnp.logical_not(final))
        def _():
            each_target(way, functools.partial(done, 0))

        each_target(way, functools.partial(done, 1))
        each_operator(way, lambda s: group_copy(way, 2, s, 1).wait_send())

    for way, sender in ((0, gives), (1, returns)):
        @pl.when(sender)
        def _():
            for d in range(1, GROUP + 1):
                chain(way, d).wait_send()


def local(blocks, transition, drive, smoother_gain, dynamics, initial_mean):
    steps, rows, dim = transition.shape
    series = initial_mean.shape[0]
    vmem = pl.BlockSpec(memory_space=pltpu.VMEM)
    hbm = pl.BlockSpec(memory_space=pltpu.HBM)
    full = pltpu.VMEM((steps, dim, dim), jnp.bfloat16)
    a_pre = pltpu.VMEM((steps, 2 * dim + 2 * PAD, dim), jnp.bfloat16)
    g_pre = pltpu.VMEM((steps + 1, 2 * dim, dim), jnp.bfloat16)
    got = pltpu.VMEM((GROUP - 1, 2 * dim, dim), jnp.bfloat16)
    group = pltpu.VMEM((GROUP - 1, PAD, dim), jnp.float32)
    means = pltpu.VMEM((steps, PAD, dim), jnp.float32)
    flat = pltpu.VMEM((steps * PAD, dim), jnp.float32)
    one = pltpu.VMEM((PAD, dim), jnp.float32)
    out = jax.ShapeDtypeStruct(drive.shape, jnp.float32)
    return pl.pallas_call(
        functools.partial(kernel, blocks, steps, rows, series),
        out_shape=(out, out),
        in_specs=[hbm] * 5,
        out_specs=(vmem, vmem),
        scratch_shapes=[
            pltpu.VMEM(drive.shape, drive.dtype),
            pltpu.VMEM(dynamics.shape, dynamics.dtype),
            pltpu.VMEM(initial_mean.shape, initial_mean.dtype),
            full, full, a_pre, g_pre, got, got, group, group, one, one,
            pltpu.VMEM((1, 2 * dim, dim), jnp.bfloat16), one,
            pltpu.VMEM((1, 2 * dim, dim), jnp.bfloat16), one,
            means, flat, means, flat,
            pltpu.VMEM((2, dim, dim), jnp.bfloat16),
            one, one, one, one,
            pltpu.SemaphoreType.DMA((5,)),
            pltpu.SemaphoreType.DMA((2, 3, steps)),
            pltpu.SemaphoreType.DMA((2, 3, steps)),
            pltpu.SemaphoreType.DMA((2, 3, GROUP - 1)),
            pltpu.SemaphoreType.DMA((2, 3, GROUP - 1)),
            pltpu.SemaphoreType.DMA((2, GROUP)),
            pltpu.SemaphoreType.DMA((2,)),
        ],
        compiler_params=pltpu.CompilerParams(
            collective_id=0, has_side_effects=True, vmem_limit_bytes=60 * 1024 * 1024
        ),
    )(transition, smoother_gain, drive, dynamics, initial_mean)


def solution(mesh):
    placed = (P("tm", "col", None), P("tm", "col", None), P("tm", "col", None), P(), P("col", None))
    return jax.shard_map(
        functools.partial(local, mesh.shape["tm"]),
        mesh=mesh,
        in_specs=placed,
        out_specs=(P("tm", "col", None), P("tm", "col", None)),
        check_vma=False,
    )
```

```python
import functools

import jax
import jax.numpy as jnp
from jax import lax
from jax.experimental import pallas as pl
from jax.experimental.pallas import tpu as pltpu
from jax.sharding import PartitionSpec as P

MESH = pl.DeviceIdType.MESH
PAD = 8
GROUP = 4


def dot(left, right):
    return jnp.dot(left, right, preferred_element_type=jnp.float32)


def halves(x):
    hi = x.astype(jnp.bfloat16)
    lo = (x - hi.astype(jnp.float32)).astype(jnp.bfloat16)
    return hi, lo


def stacked(x):
    hi = x.astype(jnp.bfloat16).astype(jnp.float32)
    return jnp.concatenate([hi, x - hi], axis=0).astype(jnp.bfloat16)


def folded(r):
    rows = r.shape[0] // 2
    return r[:rows] + r[rows:]


def kernel(
    blocks, steps, rows, series,
    a_ref, g_ref, drive_hbm, dyn_hbm, init_hbm, filt_ref, smooth_ref,
    drive_ref, dyn_ref, init_ref,
    a_full, g_full, a_pre, g_pre, a_got, g_got, v_got, b_got, v_out, b_out, e_pre, e_vec, d_pre, d_vec, u_pre,
    vst, fst, lst, pst, dyn_hl, x_out, x_in, s_out, s_in,
    local_sem, send_sem, recv_sem, group_send, group_recv, chain_send, chain_recv,
):
    dim = dyn_ref.shape[0]

    def fetch(n):
        src, dst = ((drive_hbm, drive_ref), (dyn_hbm, dyn_ref), (init_hbm, init_ref))[n]
        return pltpu.make_async_copy(src, dst, local_sem.at[2 + n])

    for n in range(3):
        fetch(n).start()
    place = lax.axis_index("tm")
    me = lax.axis_index("col")
    sib = me + 1 - 2 * lax.rem(me, 2)
    cross = lax.rem(me + 2, 4)
    q = lax.rem(place, GROUP)
    begin = place - q
    first = place == 0
    last = place == blocks - 1
    low = begin == 0
    high = begin == blocks - GROUP

    barrier = pltpu.get_barrier_semaphore()

    def greet(other):
        pl.semaphore_signal(barrier, inc=1, device_id=other, device_id_type=MESH)

    greet({"col": sib})
    greet({"col": cross})
    for d in range(1, GROUP):
        greet({"tm": begin + lax.rem(q + d, GROUP)})

    @pl.when(jnp.logical_not(high))
    def _():
        greet({"tm": begin + GROUP})

        @pl.when(q == GROUP - 1)
        def _():
            for d in range(1, GROUP):
                greet({"tm": begin + GROUP + d})

    @pl.when(jnp.logical_not(low))
    def _():
        greet({"tm": begin - 1})

        @pl.when(q == 0)
        def _():
            for d in range(1, GROUP):
                greet({"tm": begin - 1 - d})

    above = jnp.where(high, 0, jnp.where(q == GROUP - 1, GROUP, 1))
    below = jnp.where(low, 0, jnp.where(q == 0, GROUP, 1))
    pl.semaphore_wait(barrier, GROUP + 1 + above + below)

    own = pl.ds(pl.multiple_of(me * rows, rows), rows)
    passed = pl.ds(pl.multiple_of(cross * rows, rows), rows)

    def move(which, kind, t):
        source, full = ((a_ref, a_full), (g_ref, g_full))[which]
        if kind == 2:
            src = full.at[t, passed, :]
            dst = full.at[t, passed, :]
        else:
            src = source.at[t]
            dst = full.at[t, own, :]
        return pltpu.make_async_remote_copy(
            src_ref=src,
            dst_ref=dst,
            send_sem=send_sem.at[which, kind, t],
            recv_sem=recv_sem.at[which, kind, t],
            device_id={"col": cross if kind == 1 else sib},
            device_id_type=MESH,
        )

    def kept(which):
        source, full = ((a_ref, a_full), (g_ref, g_full))[which]
        return pltpu.make_async_copy(source, full.at[:, own, :], local_sem.at[which])

    for t in range(steps):
        move(0, 1, t).start()
    for t in range(steps):
        move(0, 0, t).start()
    kept(0).start()
    kept(1).start()
    half_steps = steps // 2

    def lap_steps(n):
        return steps - 1 - n, half_steps - 1 - n


    for n in range(3):
        fetch(n).wait()

    hi, lo = halves(dyn_ref[...])
    dyn_hl[0] = hi
    dyn_hl[1] = lo
    rest = jnp.zeros((PAD - series, dim), jnp.float32)

    def padded(x):
        return jnp.concatenate([x, rest], axis=0)

    def pass_on(which, t):
        move(which, 1, t).wait_recv()
        move(which, 2, t).start()

    def keep_pre(pre, t, p):
        hi, lo = halves(p)
        pre[t, 0:dim] = hi
        pre[t, dim : 2 * dim] = lo

    kept(0).wait()
    ahead = 3
    for t in range(ahead):
        pass_on(0, t)

    def arrived(which, t):
        move(which, 0, t).wait_recv()
        move(which, 2, t).wait_recv()

    arrived(0, 0)
    a_pre[0, 0:dim] = a_full[0]
    a_pre[0, dim : 2 * dim] = jnp.zeros((dim, dim), jnp.bfloat16)
    v0 = padded(drive_ref[0])
    vst[0] = v0
    a_pre[0, 2 * dim : 2 * dim + 2 * PAD] = stacked(v0)

    def forward_step(t, carry):
        @pl.when(t + ahead - 1 < steps)
        def _():
            pass_on(0, t + ahead - 1)

        @pl.when(t >= steps - half_steps)
        def _():
            for g in lap_steps(t - (steps - half_steps)):
                move(1, 1, g).start()
                move(1, 0, g).start()

        arrived(0, t)
        r = dot(a_pre[t - 1], a_full[t])
        v = folded(r[2 * dim :]) + padded(drive_ref[t])
        keep_pre(a_pre, t, r[0:dim] + r[dim : 2 * dim])
        vst[t] = v
        a_pre[t, 2 * dim : 2 * dim + 2 * PAD] = stacked(v)
        return carry

    lax.fori_loop(1, steps, forward_step, 0)

    half = lax.rem(me, 2)
    mine = pl.ds(pl.multiple_of(half * dim, dim), dim)

    def group_copy(way, kind, slot, d):
        pre, got, out, means = ((a_pre, a_got, v_out, v_got), (g_pre, g_got, b_out, b_got))[way]
        block = steps - 1 if way == 0 else steps
        if kind == 0:
            src, dst = pre.at[block, mine, :], got.at[slot, mine, :]
        elif kind == 1:
            src, dst = out, means.at[slot]
        else:
            src, dst = got.at[slot, mine, :], got.at[slot, mine, :]
        to = {"col": sib} if kind == 2 else {"tm": place + d if way == 0 else place - d}
        return pltpu.make_async_remote_copy(
            src_ref=src,
            dst_ref=dst,
            send_sem=group_send.at[way, kind, slot if kind == 2 else d - 1],
            recv_sem=group_recv.at[way, kind, slot],
            device_id=to,
            device_id_type=MESH,
        )

    def each_target(way, body):
        for d in reversed(range(1, GROUP)):
            pl.when(q + d <= GROUP - 1 if way == 0 else q >= d)(functools.partial(body, d))

    def spread(way, kind):
        slot = q if way == 0 else q - 1
        each_target(way, lambda d: group_copy(way, kind, slot, d).start())

    def each_source(way, body):
        for s in range(GROUP - 1) if way == 0 else reversed(range(GROUP - 1)):
            pl.when(q > s if way == 0 else q <= s)(functools.partial(body, s))

    def each_operator(way, body):
        for s in range(GROUP - 1) if way == 0 else reversed(range(GROUP - 1)):
            needed = q > s if way == 0 else q <= s
            if way == 0 and s == 0:
                needed = jnp.logical_and(needed, jnp.logical_not(low))
            if way == 1 and s == GROUP - 2:
                needed = jnp.logical_and(needed, jnp.logical_not(high))
            pl.when(needed)(functools.partial(body, s))

    def share(way):
        def one(s):
            group_copy(way, 0, s, 1).wait_recv()
            group_copy(way, 2, s, 1).start()

        each_operator(way, one)

    def applied(state, pre, block):
        r = dot(state, pre[block, 0:dim]) + dot(state, pre[block, dim : 2 * dim])
        return folded(r)

    @pl.when(low)
    def _():
        x_in[...] = padded(init_ref[...])

    @pl.when(first)
    def _():
        v_out[...] = applied(stacked(x_in[...]), a_pre, steps - 1) + vst[steps - 1]

    @pl.when(jnp.logical_not(first))
    def _():
        v_out[...] = vst[steps - 1]
        spread(0, 0)

    spread(0, 1)

    end = steps - 1

    def rows_of(t):
        return pl.ds(pl.multiple_of(t * PAD, PAD), PAD)

    def joined(left, i, right, j):
        r = dot(left[i, 0 : 2 * dim], right[j, 0:dim])
        more = dot(left[i, 0:dim], right[j, dim : 2 * dim])
        return r[0:dim] + r[dim : 2 * dim] + more

    def slot_of(base, i):
        return i - 1 + (0 if base == 0 else half_steps - 2)

    def gains():
        def pass_pair(n):
            for t in lap_steps(n):
                pass_on(1, t)

        pass_pair(0)
        pass_pair(1)
        kept(1).wait()
        for t in lap_steps(0):
            arrived(1, t)
            g_pre[t, 0:dim] = g_full[t]
            g_pre[t, dim : 2 * dim] = jnp.zeros((dim, dim), jnp.bfloat16)

        def lap(n, carry):
            @pl.when(n < half_steps - 1)
            def _():
                pass_pair(n + 1)

            for t in lap_steps(n):
                arrived(1, t)
                r = dot(g_pre[t + 1], g_full[t])
                keep_pre(g_pre, t, r[0:dim] + r[dim : 2 * dim])
            return carry

        lax.fori_loop(1, half_steps, lap, 0)

        @pl.when(jnp.logical_not(last))
        def _():
            keep_pre(g_pre, steps, joined(g_pre, half_steps, g_pre, 0))
            spread(1, 0)

        for i in range(1, half_steps - 1):
            for base in (half_steps, 0):
                gain = g_full[base + i]
                if i == 1:
                    p = dot(gain, g_full[base])
                else:
                    n = slot_of(base, i - 1)
                    p = dot(gain, u_pre[n, 0:dim]) + dot(gain, u_pre[n, dim : 2 * dim])
                keep_pre(u_pre, slot_of(base, i), p)

    def chain(way, d):
        src, dst = ((x_out, x_in), (s_out, s_in))[way]
        return pltpu.make_async_remote_copy(
            src_ref=src,
            dst_ref=dst,
            send_sem=chain_send.at[way, d - 1],
            recv_sem=chain_recv.at[way],
            device_id={"tm": place + d if way == 0 else place - d},
            device_id_type=MESH,
        )

    gives = jnp.logical_and(q == GROUP - 1, jnp.logical_not(high))

    def filtering():
        share(0)

        def take(s):
            group_copy(0, 1, s, 1).wait_recv()
            if s == 0:
                d_vec[...] = v_got[s]

                @pl.when(jnp.logical_not(low))
                def _():
                    group_copy(0, 2, s, 1).wait_recv()
                    d_pre[0] = a_got[s]
            else:
                group_copy(0, 2, s, 1).wait_recv()
                d_vec[...] = applied(stacked(d_vec[...]), a_got, s) + v_got[s]

                @pl.when(jnp.logical_not(low))
                def _():
                    keep_pre(d_pre, 0, joined(d_pre, 0, a_got, s))

        each_source(0, take)

        @pl.when(jnp.logical_and(low, q > 0))
        def _():
            x_in[...] = d_vec[...]

        @pl.when(jnp.logical_not(low))
        def _():
            chain(0, 1).wait_recv()

            @pl.when(q > 0)
            def _():
                x_in[...] = applied(stacked(x_in[...]), d_pre, 0) + d_vec[...]

        x = stacked(x_in[...])

        def filtered_at(t):
            f = applied(x, a_pre, t) + vst[t]
            fst[t * PAD : (t + 1) * PAD] = f
            filt_ref[t] = f[0:series]
            return f

        x_out[...] = filtered_at(end)

        @pl.when(gives)
        def _():
            for d in reversed(range(1, GROUP + 1)):
                chain(0, d).start()

        for t in range(end):
            filtered_at(t)

    hurry = jnp.logical_and(low, q == GROUP - 1)

    def phase(n, carry):
        pl.when(hurry == (n == 1))(gains)
        pl.when(n == 0)(filtering)
        return carry

    lax.fori_loop(0, 2, phase, 0)

    f_all = stacked(fst[...])
    pst[...] = folded(dot(f_all, dyn_hl[0]) + dot(f_all, dyn_hl[1]))

    def mean_step(state, t):
        moved = -pst[rows_of(t)] if state is None else state - pst[rows_of(t)]
        now = folded(dot(stacked(moved), g_full[t]))
        if t == end:
            now = jnp.where(last, jnp.zeros_like(now), now)
        now = now + fst[rows_of(t)]
        lst[t] = now
        return now

    def direct(base, top):
        total = fst[rows_of(base)]
        for i in range(half_steps):
            less = pst[rows_of(base + i)]
            if i < half_steps - 1:
                moved = stacked(fst[rows_of(base + i + 1)] - less)
                if i == 0:
                    part = folded(dot(moved, g_full[base]))
                else:
                    part = applied(moved, u_pre, slot_of(base, i))
            else:
                part = applied(stacked(-less if top is None else top - less), g_pre, base)
                if top is None:
                    part = jnp.where(last, jnp.zeros_like(part), part)
            total = total + part
        return total

    b_out[...] = direct(0, direct(half_steps, None))
    spread(1, 1)
    share(1)

    upper = lower = None
    for t_up, t_low in map(lap_steps, range(half_steps)):
        upper = mean_step(upper, t_up)
        lower = mean_step(lower, t_low)

    @pl.when(q == GROUP - 1)
    def _():
        e_vec[...] = jnp.zeros((PAD, dim), jnp.float32)

    def take_back(s):
        group_copy(1, 1, s, 1).wait_recv()
        if s == GROUP - 2:
            e_vec[...] = b_got[s]

            @pl.when(jnp.logical_not(high))
            def _():
                group_copy(1, 2, s, 1).wait_recv()
                e_pre[0] = g_got[s]
        else:
            group_copy(1, 2, s, 1).wait_recv()
            e_vec[...] = applied(stacked(e_vec[...]), g_got, s) + b_got[s]

            @pl.when(jnp.logical_not(high))
            def _():
                keep_pre(e_pre, 0, joined(e_pre, 0, g_got, s))

    each_source(1, take_back)

    @pl.when(high)
    def _():
        s_in[...] = e_vec[...]

    @pl.when(jnp.logical_not(high))
    def _():
        chain(1, 1).wait_recv()

        @pl.when(q < GROUP - 1)
        def _():
            s_in[...] = applied(stacked(s_in[...]), e_pre, 0) + e_vec[...]

    returns = jnp.logical_and(q == 0, jnp.logical_not(low))

    @pl.when(last)
    def _():
        smooth_ref[0] = b_out[0:series]
        for t in range(half_steps, steps):
            smooth_ref[t] = lst[t][0:series]

    @pl.when(jnp.logical_not(last))
    def _():
        s = stacked(s_in[...])
        now = applied(s, g_pre, steps) + b_out[...]
        s_out[...] = now
        smooth_ref[0] = now[0:series]

        @pl.when(returns)
        def _():
            for d in reversed(range(1, GROUP + 1)):
                chain(1, d).start()

        for t in range(half_steps, steps):
            now = applied(s, g_pre, t) + lst[t]
            smooth_ref[t] = now[0:series]
            if t == half_steps:
                lst[t] = now

    middle = stacked(lst[half_steps])
    for t in range(1, half_steps):
        smooth_ref[t] = (applied(middle, g_pre, t) + lst[t])[0:series]

    def sent(t, carry):
        for which in range(2):
            for kind in range(3):
                move(which, kind, t).wait_send()
        return carry

    lax.fori_loop(0, steps, sent, 0)

    for way, final in ((0, first), (1, last)):

        def done(kind, d):
            group_copy(way, kind, 0, d).wait_send()

        @pl.when(jnp.logical_not(final))
        def _():
            each_target(way, functools.partial(done, 0))

        each_target(way, functools.partial(done, 1))
        each_operator(way, lambda s: group_copy(way, 2, s, 1).wait_send())

    for way, sender in ((0, gives), (1, returns)):
        @pl.when(sender)
        def _():
            for d in range(1, GROUP + 1):
                chain(way, d).wait_send()


def local(blocks, transition, drive, smoother_gain, dynamics, initial_mean):
    steps, rows, dim = transition.shape
    series = initial_mean.shape[0]
    vmem = pl.BlockSpec(memory_space=pltpu.VMEM)
    hbm = pl.BlockSpec(memory_space=pltpu.HBM)
    full = pltpu.VMEM((steps, dim, dim), jnp.bfloat16)
    a_pre = pltpu.VMEM((steps, 2 * dim + 2 * PAD, dim), jnp.bfloat16)
    g_pre = pltpu.VMEM((steps + 1, 2 * dim, dim), jnp.bfloat16)
    got = pltpu.VMEM((GROUP - 1, 2 * dim, dim), jnp.bfloat16)
    group = pltpu.VMEM((GROUP - 1, PAD, dim), jnp.float32)
    means = pltpu.VMEM((steps, PAD, dim), jnp.float32)
    flat = pltpu.VMEM((steps * PAD, dim), jnp.float32)
    one = pltpu.VMEM((PAD, dim), jnp.float32)
    out = jax.ShapeDtypeStruct(drive.shape, jnp.float32)
    pinned = [
        pltpu.with_memory_space_constraint(x, pltpu.HBM)
        for x in (transition, smoother_gain, drive, dynamics, initial_mean)
    ]
    return pl.pallas_call(
        functools.partial(kernel, blocks, steps, rows, series),
        out_shape=(out, out),
        in_specs=[hbm] * 5,
        out_specs=(vmem, vmem),
        scratch_shapes=[
            pltpu.VMEM(drive.shape, drive.dtype),
            pltpu.VMEM(dynamics.shape, dynamics.dtype),
            pltpu.VMEM(initial_mean.shape, initial_mean.dtype),
            full, full, a_pre, g_pre, got, got, group, group, one, one,
            pltpu.VMEM((1, 2 * dim, dim), jnp.bfloat16), one,
            pltpu.VMEM((1, 2 * dim, dim), jnp.bfloat16), one,
            pltpu.VMEM((steps - 4, 2 * dim, dim), jnp.bfloat16),
            means, flat, means, flat,
            pltpu.VMEM((2, dim, dim), jnp.bfloat16),
            one, one, one, one,
            pltpu.SemaphoreType.DMA((5,)),
            pltpu.SemaphoreType.DMA((2, 3, steps)),
            pltpu.SemaphoreType.DMA((2, 3, steps)),
            pltpu.SemaphoreType.DMA((2, 3, GROUP - 1)),
            pltpu.SemaphoreType.DMA((2, 3, GROUP - 1)),
            pltpu.SemaphoreType.DMA((2, GROUP)),
            pltpu.SemaphoreType.DMA((2,)),
        ],
        compiler_params=pltpu.CompilerParams(
            collective_id=0, has_side_effects=True, vmem_limit_bytes=40 * 1024 * 1024
        ),
    )(*pinned)


def solution(mesh):
    placed = (P("tm", "col", None), P("tm", "col", None), P("tm", "col", None), P(), P("col", None))
    return jax.shard_map(
        functools.partial(local, mesh.shape["tm"]),
        mesh=mesh,
        in_specs=placed,
        out_specs=(P("tm", "col", None), P("tm", "col", None)),
        check_vma=False,
    )
```

```python
import functools

import jax
import jax.numpy as jnp
from jax import lax
from jax.experimental import pallas as pl
from jax.experimental.pallas import tpu as pltpu
from jax.sharding import PartitionSpec as P

MESH = pl.DeviceIdType.MESH
PAD = 8
GROUP = 4


def dot(left, right):
    return jnp.dot(left, right, preferred_element_type=jnp.float32)


def halves(x):
    hi = x.astype(jnp.bfloat16)
    lo = (x - hi.astype(jnp.float32)).astype(jnp.bfloat16)
    return hi, lo


def stacked(x):
    hi = x.astype(jnp.bfloat16).astype(jnp.float32)
    return jnp.concatenate([hi, x - hi], axis=0).astype(jnp.bfloat16)


def folded(r):
    rows = r.shape[0] // 2
    return r[:rows] + r[rows:]


def kernel(
    blocks, steps, rows, series,
    a_ref, g_ref, drive_hbm, dyn_hbm, init_hbm, filt_ref, smooth_ref,
    drive_ref, dyn_ref, init_ref,
    a_full, g_full, a_pre, g_pre, a_got, g_got, v_got, b_got, v_out, b_out, e_pre, e_vec, d_pre, d_vec, u_pre,
    vst, fst, lst, pst, dyn_hl, x_out, x_in, s_out, s_in,
    local_sem, send_sem, recv_sem, group_send, group_recv, chain_send, chain_recv,
):
    dim = dyn_ref.shape[0]

    def fetch(n):
        src, dst = ((drive_hbm, drive_ref), (dyn_hbm, dyn_ref), (init_hbm, init_ref))[n]
        return pltpu.make_async_copy(src, dst, local_sem.at[2 + n])

    for n in range(3):
        fetch(n).start()
    place = lax.axis_index("tm")
    me = lax.axis_index("col")
    sib = me + 1 - 2 * lax.rem(me, 2)
    cross = lax.rem(me + 2, 4)
    q = lax.rem(place, GROUP)
    begin = place - q
    first = place == 0
    last = place == blocks - 1
    low = begin == 0
    high = begin == blocks - GROUP

    barrier = pltpu.get_barrier_semaphore()

    def greet(other):
        pl.semaphore_signal(barrier, inc=1, device_id=other, device_id_type=MESH)

    greet({"col": sib})
    greet({"col": cross})
    for d in range(1, GROUP):
        greet({"tm": begin + lax.rem(q + d, GROUP)})

    @pl.when(jnp.logical_not(high))
    def _():
        greet({"tm": begin + GROUP})

        @pl.when(q == GROUP - 1)
        def _():
            for d in range(1, GROUP):
                greet({"tm": begin + GROUP + d})

    @pl.when(jnp.logical_not(low))
    def _():
        greet({"tm": begin - 1})

        @pl.when(q == 0)
        def _():
            for d in range(1, GROUP):
                greet({"tm": begin - 1 - d})

    above = jnp.where(high, 0, jnp.where(q == GROUP - 1, GROUP, 1))
    below = jnp.where(low, 0, jnp.where(q == 0, GROUP, 1))
    pl.semaphore_wait(barrier, GROUP + 1 + above + below)

    own = pl.ds(pl.multiple_of(me * rows, rows), rows)
    passed = pl.ds(pl.multiple_of(cross * rows, rows), rows)

    def move(which, kind, t):
        source, full = ((a_ref, a_full), (g_ref, g_full))[which]
        if kind == 2:
            src = full.at[t, passed, :]
            dst = full.at[t, passed, :]
        else:
            src = source.at[t]
            dst = full.at[t, own, :]
        return pltpu.make_async_remote_copy(
            src_ref=src,
            dst_ref=dst,
            send_sem=send_sem.at[which, kind, t],
            recv_sem=recv_sem.at[which, kind, t],
            device_id={"col": cross if kind == 1 else sib},
            device_id_type=MESH,
        )

    def kept(which):
        source, full = ((a_ref, a_full), (g_ref, g_full))[which]
        return pltpu.make_async_copy(source, full.at[:, own, :], local_sem.at[which])

    for t in range(steps):
        move(0, 1, t).start()
    for t in range(steps):
        move(0, 0, t).start()
    kept(0).start()
    kept(1).start()
    half_steps = steps // 2

    def lap_steps(n):
        return steps - 1 - n, half_steps - 1 - n


    for n in range(3):
        fetch(n).wait()

    hi, lo = halves(dyn_ref[...])
    dyn_hl[0] = hi
    dyn_hl[1] = lo
    rest = jnp.zeros((PAD - series, dim), jnp.float32)

    def padded(x):
        return jnp.concatenate([x, rest], axis=0)

    def pass_on(which, t):
        move(which, 1, t).wait_recv()
        move(which, 2, t).start()

    def keep_pre(pre, t, p):
        hi, lo = halves(p)
        pre[t, 0:dim] = hi
        pre[t, dim : 2 * dim] = lo

    kept(0).wait()
    ahead = 3
    for t in range(ahead):
        pass_on(0, t)

    def arrived(which, t):
        move(which, 0, t).wait_recv()
        move(which, 2, t).wait_recv()

    arrived(0, 0)
    a_pre[0, 0:dim] = a_full[0]
    a_pre[0, dim : 2 * dim] = jnp.zeros((dim, dim), jnp.bfloat16)
    v0 = padded(drive_ref[0])
    vst[0] = v0
    a_pre[0, 2 * dim : 2 * dim + 2 * PAD] = stacked(v0)

    def forward_step(t, carry):
        @pl.when(t + ahead - 1 < steps)
        def _():
            pass_on(0, t + ahead - 1)

        @pl.when(t >= steps - half_steps)
        def _():
            for g in lap_steps(t - (steps - half_steps)):
                move(1, 1, g).start()
                move(1, 0, g).start()

        arrived(0, t)
        r = dot(a_pre[t - 1], a_full[t])
        v = folded(r[2 * dim :]) + padded(drive_ref[t])
        keep_pre(a_pre, t, r[0:dim] + r[dim : 2 * dim])
        vst[t] = v
        a_pre[t, 2 * dim : 2 * dim + 2 * PAD] = stacked(v)
        return carry

    lax.fori_loop(1, steps, forward_step, 0)

    half = lax.rem(me, 2)
    mine = pl.ds(pl.multiple_of(half * dim, dim), dim)

    def group_copy(way, kind, slot, d):
        pre, got, out, means = ((a_pre, a_got, v_out, v_got), (g_pre, g_got, b_out, b_got))[way]
        block = steps - 1 if way == 0 else steps
        if kind == 0:
            src, dst = pre.at[block, mine, :], got.at[slot, mine, :]
        elif kind == 1:
            src, dst = out, means.at[slot]
        else:
            src, dst = got.at[slot, mine, :], got.at[slot, mine, :]
        to = {"col": sib} if kind == 2 else {"tm": place + d if way == 0 else place - d}
        return pltpu.make_async_remote_copy(
            src_ref=src,
            dst_ref=dst,
            send_sem=group_send.at[way, kind, slot if kind == 2 else d - 1],
            recv_sem=group_recv.at[way, kind, slot],
            device_id=to,
            device_id_type=MESH,
        )

    def each_target(way, body):
        for d in reversed(range(1, GROUP)):
            pl.when(q + d <= GROUP - 1 if way == 0 else q >= d)(functools.partial(body, d))

    def spread(way, kind):
        slot = q if way == 0 else q - 1
        each_target(way, lambda d: group_copy(way, kind, slot, d).start())

    def each_source(way, body):
        for s in range(GROUP - 1) if way == 0 else reversed(range(GROUP - 1)):
            pl.when(q > s if way == 0 else q <= s)(functools.partial(body, s))

    def each_operator(way, body):
        for s in range(GROUP - 1) if way == 0 else reversed(range(GROUP - 1)):
            needed = q > s if way == 0 else q <= s
            if way == 0 and s == 0:
                needed = jnp.logical_and(needed, jnp.logical_not(low))
            if way == 1 and s == GROUP - 2:
                needed = jnp.logical_and(needed, jnp.logical_not(high))
            pl.when(needed)(functools.partial(body, s))

    def share(way):
        def one(s):
            group_copy(way, 0, s, 1).wait_recv()
            group_copy(way, 2, s, 1).start()

        each_operator(way, one)

    def applied(state, pre, block):
        r = dot(state, pre[block, 0:dim]) + dot(state, pre[block, dim : 2 * dim])
        return folded(r)

    @pl.when(low)
    def _():
        x_in[...] = padded(init_ref[...])

    @pl.when(first)
    def _():
        v_out[...] = applied(stacked(x_in[...]), a_pre, steps - 1) + vst[steps - 1]

    @pl.when(jnp.logical_not(first))
    def _():
        v_out[...] = vst[steps - 1]
        spread(0, 0)

    spread(0, 1)

    end = steps - 1

    def rows_of(t):
        return pl.ds(pl.multiple_of(t * PAD, PAD), PAD)

    def joined(left, i, right, j):
        r = dot(left[i, 0 : 2 * dim], right[j, 0:dim])
        more = dot(left[i, 0:dim], right[j, dim : 2 * dim])
        return r[0:dim] + r[dim : 2 * dim] + more

    def slot_of(base, i):
        return i - 1 + (0 if base == 0 else half_steps - 2)

    def gains():
        def pass_pair(n):
            for t in lap_steps(n):
                pass_on(1, t)

        pass_pair(0)
        pass_pair(1)
        kept(1).wait()
        for t in lap_steps(0):
            arrived(1, t)
            g_pre[t, 0:dim] = g_full[t]
            g_pre[t, dim : 2 * dim] = jnp.zeros((dim, dim), jnp.bfloat16)

        def lap(n, carry):
            @pl.when(n < half_steps - 1)
            def _():
                pass_pair(n + 1)

            for t in lap_steps(n):
                arrived(1, t)
                r = dot(g_pre[t + 1], g_full[t])
                keep_pre(g_pre, t, r[0:dim] + r[dim : 2 * dim])
            return carry

        lax.fori_loop(1, half_steps, lap, 0)

        @pl.when(jnp.logical_not(last))
        def _():
            keep_pre(g_pre, steps, joined(g_pre, half_steps, g_pre, 0))
            spread(1, 0)

        for i in range(1, half_steps - 1):
            for base in (half_steps, 0):
                gain = g_full[base + i]
                if i == 1:
                    p = dot(gain, g_full[base])
                else:
                    n = slot_of(base, i - 1)
                    p = dot(gain, u_pre[n, 0:dim]) + dot(gain, u_pre[n, dim : 2 * dim])
                keep_pre(u_pre, slot_of(base, i), p)

    def chain(way, d):
        src, dst = ((x_out, x_in), (s_out, s_in))[way]
        return pltpu.make_async_remote_copy(
            src_ref=src,
            dst_ref=dst,
            send_sem=chain_send.at[way, d - 1],
            recv_sem=chain_recv.at[way],
            device_id={"tm": place + d if way == 0 else place - d},
            device_id_type=MESH,
        )

    gives = jnp.logical_and(q == GROUP - 1, jnp.logical_not(high))

    def filtering():
        share(0)

        def take(s):
            group_copy(0, 1, s, 1).wait_recv()
            if s == 0:
                d_vec[...] = v_got[s]

                @pl.when(jnp.logical_not(low))
                def _():
                    group_copy(0, 2, s, 1).wait_recv()
                    d_pre[0] = a_got[s]
            else:
                group_copy(0, 2, s, 1).wait_recv()
                d_vec[...] = applied(stacked(d_vec[...]), a_got, s) + v_got[s]

                @pl.when(jnp.logical_not(low))
                def _():
                    keep_pre(d_pre, 0, joined(d_pre, 0, a_got, s))

        each_source(0, take)

        @pl.when(jnp.logical_and(low, q > 0))
        def _():
            x_in[...] = d_vec[...]

        @pl.when(jnp.logical_not(low))
        def _():
            chain(0, 1).wait_recv()

            @pl.when(q > 0)
            def _():
                x_in[...] = applied(stacked(x_in[...]), d_pre, 0) + d_vec[...]

        x = stacked(x_in[...])

        def filtered_at(t):
            f = applied(x, a_pre, t) + vst[t]
            fst[t * PAD : (t + 1) * PAD] = f
            filt_ref[t] = f[0:series]
            return f

        x_out[...] = filtered_at(end)

        @pl.when(gives)
        def _():
            for d in reversed(range(1, GROUP + 1)):
                chain(0, d).start()

        for t in range(end):
            filtered_at(t)

    hurry = jnp.logical_and(low, q == GROUP - 1)

    def phase(n, carry):
        pl.when(hurry == (n == 1))(gains)
        pl.when(n == 0)(filtering)
        return carry

    lax.fori_loop(0, 2, phase, 0)

    f_all = stacked(fst[...])
    pst[...] = folded(dot(f_all, dyn_hl[0]) + dot(f_all, dyn_hl[1]))

    def mean_step(state, t):
        moved = -pst[rows_of(t)] if state is None else state - pst[rows_of(t)]
        now = folded(dot(stacked(moved), g_full[t]))
        if t == end:
            now = jnp.where(last, jnp.zeros_like(now), now)
        now = now + fst[rows_of(t)]
        lst[t] = now
        return now

    def direct(base, top):
        total = fst[rows_of(base)]
        for i in range(half_steps):
            less = pst[rows_of(base + i)]
            if i < half_steps - 1:
                moved = stacked(fst[rows_of(base + i + 1)] - less)
                if i == 0:
                    part = folded(dot(moved, g_full[base]))
                else:
                    part = applied(moved, u_pre, slot_of(base, i))
            else:
                part = applied(stacked(-less if top is None else top - less), g_pre, base)
                if top is None:
                    part = jnp.where(last, jnp.zeros_like(part), part)
            total = total + part
        return total

    b_out[...] = direct(0, direct(half_steps, None))
    spread(1, 1)
    share(1)

    upper = lower = None
    for t_up, t_low in map(lap_steps, range(half_steps)):
        upper = mean_step(upper, t_up)
        lower = mean_step(lower, t_low)

    @pl.when(q == GROUP - 1)
    def _():
        e_vec[...] = jnp.zeros((PAD, dim), jnp.float32)

    def take_back(s):
        group_copy(1, 1, s, 1).wait_recv()
        if s == GROUP - 2:
            e_vec[...] = b_got[s]

            @pl.when(jnp.logical_not(high))
            def _():
                group_copy(1, 2, s, 1).wait_recv()
                e_pre[0] = g_got[s]
        else:
            group_copy(1, 2, s, 1).wait_recv()
            e_vec[...] = applied(stacked(e_vec[...]), g_got, s) + b_got[s]

            @pl.when(jnp.logical_not(high))
            def _():
                keep_pre(e_pre, 0, joined(e_pre, 0, g_got, s))

    each_source(1, take_back)

    def settle():
        def sent(t, carry):
            for which in range(2):
                for kind in range(3):
                    move(which, kind, t).wait_send()
            return carry

        lax.fori_loop(0, steps, sent, 0)

        for way, final in ((0, first), (1, last)):

            def done(kind, d):
                group_copy(way, kind, 0, d).wait_send()

            @pl.when(jnp.logical_not(final))
            def _():
                each_target(way, functools.partial(done, 0))

            each_target(way, functools.partial(done, 1))
            each_operator(way, lambda s: group_copy(way, 2, s, 1).wait_send())

    pl.when(low)(settle)

    @pl.when(high)
    def _():
        s_in[...] = e_vec[...]

    @pl.when(jnp.logical_not(high))
    def _():
        chain(1, 1).wait_recv()

        @pl.when(q < GROUP - 1)
        def _():
            s_in[...] = applied(stacked(s_in[...]), e_pre, 0) + e_vec[...]

    returns = jnp.logical_and(q == 0, jnp.logical_not(low))

    @pl.when(last)
    def _():
        smooth_ref[0] = b_out[0:series]
        for t in range(half_steps, steps):
            smooth_ref[t] = lst[t][0:series]

    @pl.when(jnp.logical_not(last))
    def _():
        s = stacked(s_in[...])
        now = applied(s, g_pre, steps) + b_out[...]
        s_out[...] = now
        smooth_ref[0] = now[0:series]

        @pl.when(returns)
        def _():
            for d in reversed(range(1, GROUP + 1)):
                chain(1, d).start()

        for t in range(half_steps, steps):
            now = applied(s, g_pre, t) + lst[t]
            smooth_ref[t] = now[0:series]
            if t == half_steps:
                lst[t] = now

    middle = stacked(lst[half_steps])
    for t in range(1, half_steps):
        smooth_ref[t] = (applied(middle, g_pre, t) + lst[t])[0:series]

    pl.when(jnp.logical_not(low))(settle)

    for way, sender in ((0, gives), (1, returns)):
        @pl.when(sender)
        def _():
            for d in range(1, GROUP + 1):
                chain(way, d).wait_send()


def local(blocks, transition, drive, smoother_gain, dynamics, initial_mean):
    steps, rows, dim = transition.shape
    series = initial_mean.shape[0]
    vmem = pl.BlockSpec(memory_space=pltpu.VMEM)
    hbm = pl.BlockSpec(memory_space=pltpu.HBM)
    full = pltpu.VMEM((steps, dim, dim), jnp.bfloat16)
    a_pre = pltpu.VMEM((steps, 2 * dim + 2 * PAD, dim), jnp.bfloat16)
    g_pre = pltpu.VMEM((steps + 1, 2 * dim, dim), jnp.bfloat16)
    got = pltpu.VMEM((GROUP - 1, 2 * dim, dim), jnp.bfloat16)
    group = pltpu.VMEM((GROUP - 1, PAD, dim), jnp.float32)
    means = pltpu.VMEM((steps, PAD, dim), jnp.float32)
    flat = pltpu.VMEM((steps * PAD, dim), jnp.float32)
    one = pltpu.VMEM((PAD, dim), jnp.float32)
    out = jax.ShapeDtypeStruct(drive.shape, jnp.float32)
    pinned = [
        pltpu.with_memory_space_constraint(x, pltpu.HBM)
        for x in (transition, smoother_gain, drive, dynamics, initial_mean)
    ]
    return pl.pallas_call(
        functools.partial(kernel, blocks, steps, rows, series),
        out_shape=(out, out),
        in_specs=[hbm] * 5,
        out_specs=(vmem, vmem),
        scratch_shapes=[
            pltpu.VMEM(drive.shape, drive.dtype),
            pltpu.VMEM(dynamics.shape, dynamics.dtype),
            pltpu.VMEM(initial_mean.shape, initial_mean.dtype),
            full, full, a_pre, g_pre, got, got, group, group, one, one,
            pltpu.VMEM((1, 2 * dim, dim), jnp.bfloat16), one,
            pltpu.VMEM((1, 2 * dim, dim), jnp.bfloat16), one,
            pltpu.VMEM((steps - 4, 2 * dim, dim), jnp.bfloat16),
            means, flat, means, flat,
            pltpu.VMEM((2, dim, dim), jnp.bfloat16),
            one, one, one, one,
            pltpu.SemaphoreType.DMA((5,)),
            pltpu.SemaphoreType.DMA((2, 3, steps)),
            pltpu.SemaphoreType.DMA((2, 3, steps)),
            pltpu.SemaphoreType.DMA((2, 3, GROUP - 1)),
            pltpu.SemaphoreType.DMA((2, 3, GROUP - 1)),
            pltpu.SemaphoreType.DMA((2, GROUP)),
            pltpu.SemaphoreType.DMA((2,)),
        ],
        compiler_params=pltpu.CompilerParams(
            collective_id=0, has_side_effects=True, vmem_limit_bytes=40 * 1024 * 1024
        ),
    )(*pinned)


def solution(mesh):
    placed = (P("tm", "col", None), P("tm", "col", None), P("tm", "col", None), P(), P("col", None))
    return jax.shard_map(
        functools.partial(local, mesh.shape["tm"]),
        mesh=mesh,
        in_specs=placed,
        out_specs=(P("tm", "col", None), P("tm", "col", None)),
        check_vma=False,
    )
```

```python
import functools

import jax
import jax.numpy as jnp
from jax import lax
from jax.experimental import pallas as pl
from jax.experimental.pallas import tpu as pltpu
from jax.sharding import PartitionSpec as P

MESH = pl.DeviceIdType.MESH
PAD = 8
GROUP = 4


def dot(left, right):
    return jnp.dot(left, right, preferred_element_type=jnp.float32)


def halves(x):
    hi = x.astype(jnp.bfloat16)
    lo = (x - hi.astype(jnp.float32)).astype(jnp.bfloat16)
    return hi, lo


def stacked(x):
    hi = x.astype(jnp.bfloat16).astype(jnp.float32)
    return jnp.concatenate([hi, x - hi], axis=0).astype(jnp.bfloat16)


def folded(r):
    rows = r.shape[0] // 2
    return r[:rows] + r[rows:]


def kernel(
    blocks, steps, rows, series,
    a_ref, g_ref, drive_hbm, dyn_hbm, init_hbm, filt_ref, smooth_ref,
    drive_ref, dyn_ref, init_ref,
    a_full, g_full, a_pre, g_pre, a_got, g_got, v_got, b_got, v_out, b_out, e_pre, e_vec, d_pre, d_vec, u_pre,
    vst, fst, lst, pst, dyn_hl, x_out, x_in, s_out, s_in,
    local_sem, send_sem, recv_sem, group_send, group_recv, chain_send, chain_recv,
):
    dim = dyn_ref.shape[0]

    def fetch(n):
        src, dst = ((drive_hbm, drive_ref), (dyn_hbm, dyn_ref), (init_hbm, init_ref))[n]
        return pltpu.make_async_copy(src, dst, local_sem.at[2 + n])

    for n in range(3):
        fetch(n).start()
    place = lax.axis_index("tm")
    me = lax.axis_index("col")
    sib = me + 1 - 2 * lax.rem(me, 2)
    cross = lax.rem(me + 2, 4)
    q = lax.rem(place, GROUP)
    begin = place - q
    first = place == 0
    last = place == blocks - 1
    low = begin == 0
    high = begin == blocks - GROUP

    barrier = pltpu.get_barrier_semaphore()

    def greet(other):
        pl.semaphore_signal(barrier, inc=1, device_id=other, device_id_type=MESH)

    greet({"col": sib})
    greet({"col": cross})
    for d in range(1, GROUP):
        greet({"tm": begin + lax.rem(q + d, GROUP)})

    @pl.when(jnp.logical_not(high))
    def _():
        greet({"tm": begin + GROUP})

        @pl.when(q == GROUP - 1)
        def _():
            for d in range(1, GROUP):
                greet({"tm": begin + GROUP + d})

    @pl.when(jnp.logical_not(low))
    def _():
        greet({"tm": begin - 1})

        @pl.when(q == 0)
        def _():
            for d in range(1, GROUP):
                greet({"tm": begin - 1 - d})

    above = jnp.where(high, 0, jnp.where(q == GROUP - 1, GROUP, 1))
    below = jnp.where(low, 0, jnp.where(q == 0, GROUP, 1))
    pl.semaphore_wait(barrier, GROUP + 1 + above + below)

    own = pl.ds(pl.multiple_of(me * rows, rows), rows)
    passed = pl.ds(pl.multiple_of(cross * rows, rows), rows)

    def move(which, kind, t):
        source, full = ((a_ref, a_full), (g_ref, g_full))[which]
        if kind == 2:
            src = full.at[t, passed, :]
            dst = full.at[t, passed, :]
        else:
            src = source.at[t]
            dst = full.at[t, own, :]
        return pltpu.make_async_remote_copy(
            src_ref=src,
            dst_ref=dst,
            send_sem=send_sem.at[which, kind, t],
            recv_sem=recv_sem.at[which, kind, t],
            device_id={"col": cross if kind == 1 else sib},
            device_id_type=MESH,
        )

    def kept(which):
        source, full = ((a_ref, a_full), (g_ref, g_full))[which]
        return pltpu.make_async_copy(source, full.at[:, own, :], local_sem.at[which])

    for t in range(steps):
        move(0, 1, t).start()
    for t in range(steps):
        move(0, 0, t).start()
    kept(0).start()
    kept(1).start()
    half_steps = steps // 2

    def lap_steps(n):
        return steps - 1 - n, half_steps - 1 - n


    for n in range(3):
        fetch(n).wait()

    hi, lo = halves(dyn_ref[...])
    dyn_hl[0] = hi
    dyn_hl[1] = lo
    rest = jnp.zeros((PAD - series, dim), jnp.float32)

    def padded(x):
        return jnp.concatenate([x, rest], axis=0)

    def pass_on(which, t):
        move(which, 1, t).wait_recv()
        move(which, 2, t).start()

    def keep_pre(pre, t, p):
        hi, lo = halves(p)
        pre[t, 0:dim] = hi
        pre[t, dim : 2 * dim] = lo

    kept(0).wait()
    ahead = 3
    for t in range(ahead):
        pass_on(0, t)

    def arrived(which, t):
        move(which, 0, t).wait_recv()
        move(which, 2, t).wait_recv()

    arrived(0, 0)
    a_pre[0, 0:dim] = a_full[0]
    a_pre[0, dim : 2 * dim] = jnp.zeros((dim, dim), jnp.bfloat16)
    v0 = padded(drive_ref[0])
    vst[0] = v0
    a_pre[0, 2 * dim : 2 * dim + 2 * PAD] = stacked(v0)

    def forward_step(t, carry):
        @pl.when(t + ahead - 1 < steps)
        def _():
            pass_on(0, t + ahead - 1)

        @pl.when(jnp.logical_and(t >= 2, t < 2 + half_steps))
        def _():
            for g in lap_steps(t - 2):
                move(1, 1, g).start()
                move(1, 0, g).start()

        arrived(0, t)
        r = dot(a_pre[t - 1], a_full[t])
        v = folded(r[2 * dim :]) + padded(drive_ref[t])
        keep_pre(a_pre, t, r[0:dim] + r[dim : 2 * dim])
        vst[t] = v
        a_pre[t, 2 * dim : 2 * dim + 2 * PAD] = stacked(v)
        return carry

    lax.fori_loop(1, steps, forward_step, 0)

    half = lax.rem(me, 2)
    mine = pl.ds(pl.multiple_of(half * dim, dim), dim)

    def group_copy(way, kind, slot, d):
        pre, got, out, means = ((a_pre, a_got, v_out, v_got), (g_pre, g_got, b_out, b_got))[way]
        block = steps - 1 if way == 0 else steps
        if kind == 0:
            src, dst = pre.at[block, mine, :], got.at[slot, mine, :]
        elif kind == 1:
            src, dst = out, means.at[slot]
        else:
            src, dst = got.at[slot, mine, :], got.at[slot, mine, :]
        to = {"col": sib} if kind == 2 else {"tm": place + d if way == 0 else place - d}
        return pltpu.make_async_remote_copy(
            src_ref=src,
            dst_ref=dst,
            send_sem=group_send.at[way, kind, slot if kind == 2 else d - 1],
            recv_sem=group_recv.at[way, kind, slot],
            device_id=to,
            device_id_type=MESH,
        )

    def each_target(way, body):
        for d in reversed(range(1, GROUP)):
            pl.when(q + d <= GROUP - 1 if way == 0 else q >= d)(functools.partial(body, d))

    def spread(way, kind):
        slot = q if way == 0 else q - 1
        each_target(way, lambda d: group_copy(way, kind, slot, d).start())

    def each_source(way, body):
        for s in range(GROUP - 1) if way == 0 else reversed(range(GROUP - 1)):
            pl.when(q > s if way == 0 else q <= s)(functools.partial(body, s))

    def each_operator(way, body):
        for s in range(GROUP - 1) if way == 0 else reversed(range(GROUP - 1)):
            needed = q > s if way == 0 else q <= s
            if way == 0 and s == 0:
                needed = jnp.logical_and(needed, jnp.logical_not(low))
            if way == 1 and s == GROUP - 2:
                needed = jnp.logical_and(needed, jnp.logical_not(high))
            pl.when(needed)(functools.partial(body, s))

    def share(way):
        def one(s):
            group_copy(way, 0, s, 1).wait_recv()
            group_copy(way, 2, s, 1).start()

        each_operator(way, one)

    def applied(state, pre, block):
        r = dot(state, pre[block, 0:dim]) + dot(state, pre[block, dim : 2 * dim])
        return folded(r)

    @pl.when(low)
    def _():
        x_in[...] = padded(init_ref[...])

    @pl.when(first)
    def _():
        v_out[...] = applied(stacked(x_in[...]), a_pre, steps - 1) + vst[steps - 1]

    @pl.when(jnp.logical_not(first))
    def _():
        v_out[...] = vst[steps - 1]
        spread(0, 0)

    spread(0, 1)

    end = steps - 1

    def rows_of(t):
        return pl.ds(pl.multiple_of(t * PAD, PAD), PAD)

    def joined(left, i, right, j):
        r = dot(left[i, 0 : 2 * dim], right[j, 0:dim])
        more = dot(left[i, 0:dim], right[j, dim : 2 * dim])
        return r[0:dim] + r[dim : 2 * dim] + more

    def slot_of(base, i):
        return i - 1 + (0 if base == 0 else half_steps - 2)

    def gains():
        def pass_pair(n):
            for t in lap_steps(n):
                pass_on(1, t)

        pass_pair(0)
        pass_pair(1)
        kept(1).wait()
        for t in lap_steps(0):
            arrived(1, t)
            g_pre[t, 0:dim] = g_full[t]
            g_pre[t, dim : 2 * dim] = jnp.zeros((dim, dim), jnp.bfloat16)

        def lap(n, carry):
            @pl.when(n < half_steps - 1)
            def _():
                pass_pair(n + 1)

            for t in lap_steps(n):
                arrived(1, t)
                r = dot(g_pre[t + 1], g_full[t])
                keep_pre(g_pre, t, r[0:dim] + r[dim : 2 * dim])
            return carry

        lax.fori_loop(1, half_steps, lap, 0)

        @pl.when(jnp.logical_not(last))
        def _():
            keep_pre(g_pre, steps, joined(g_pre, half_steps, g_pre, 0))
            spread(1, 0)

        for i in range(1, half_steps - 1):
            for base in (half_steps, 0):
                gain = g_full[base + i]
                if i == 1:
                    p = dot(gain, g_full[base])
                else:
                    n = slot_of(base, i - 1)
                    p = dot(gain, u_pre[n, 0:dim]) + dot(gain, u_pre[n, dim : 2 * dim])
                keep_pre(u_pre, slot_of(base, i), p)

    def chain(way, d):
        src, dst = ((x_out, x_in), (s_out, s_in))[way]
        return pltpu.make_async_remote_copy(
            src_ref=src,
            dst_ref=dst,
            send_sem=chain_send.at[way, d - 1],
            recv_sem=chain_recv.at[way],
            device_id={"tm": place + d if way == 0 else place - d},
            device_id_type=MESH,
        )

    gives = jnp.logical_and(q == GROUP - 1, jnp.logical_not(high))

    def filtering():
        share(0)

        def take(s):
            group_copy(0, 1, s, 1).wait_recv()
            if s == 0:
                d_vec[...] = v_got[s]

                @pl.when(jnp.logical_not(low))
                def _():
                    group_copy(0, 2, s, 1).wait_recv()
                    d_pre[0] = a_got[s]
            else:
                group_copy(0, 2, s, 1).wait_recv()
                d_vec[...] = applied(stacked(d_vec[...]), a_got, s) + v_got[s]

                @pl.when(jnp.logical_not(low))
                def _():
                    keep_pre(d_pre, 0, joined(d_pre, 0, a_got, s))

        each_source(0, take)

        @pl.when(jnp.logical_and(low, q > 0))
        def _():
            x_in[...] = d_vec[...]

        @pl.when(jnp.logical_not(low))
        def _():
            chain(0, 1).wait_recv()

            @pl.when(q > 0)
            def _():
                x_in[...] = applied(stacked(x_in[...]), d_pre, 0) + d_vec[...]

        x = stacked(x_in[...])

        def filtered_at(t):
            f = applied(x, a_pre, t) + vst[t]
            fst[t * PAD : (t + 1) * PAD] = f
            filt_ref[t] = f[0:series]
            return f

        x_out[...] = filtered_at(end)

        @pl.when(gives)
        def _():
            for d in reversed(range(1, GROUP + 1)):
                chain(0, d).start()

        for t in range(end):
            filtered_at(t)

    hurry = jnp.logical_and(low, q == GROUP - 1)

    def phase(n, carry):
        pl.when(hurry == (n == 1))(gains)
        pl.when(n == 0)(filtering)
        return carry

    lax.fori_loop(0, 2, phase, 0)

    f_all = stacked(fst[...])
    pst[...] = folded(dot(f_all, dyn_hl[0]) + dot(f_all, dyn_hl[1]))

    def mean_step(state, t):
        moved = -pst[rows_of(t)] if state is None else state - pst[rows_of(t)]
        now = folded(dot(stacked(moved), g_full[t]))
        if t == end:
            now = jnp.where(last, jnp.zeros_like(now), now)
        now = now + fst[rows_of(t)]
        lst[t] = now
        return now

    def direct(base, top):
        total = fst[rows_of(base)]
        for i in range(half_steps):
            less = pst[rows_of(base + i)]
            if i < half_steps - 1:
                moved = stacked(fst[rows_of(base + i + 1)] - less)
                if i == 0:
                    part = folded(dot(moved, g_full[base]))
                else:
                    part = applied(moved, u_pre, slot_of(base, i))
            else:
                part = applied(stacked(-less if top is None else top - less), g_pre, base)
                if top is None:
                    part = jnp.where(last, jnp.zeros_like(part), part)
            total = total + part
        return total

    b_out[...] = direct(0, direct(half_steps, None))
    spread(1, 1)
    share(1)

    upper = lower = None
    for t_up, t_low in map(lap_steps, range(half_steps)):
        upper = mean_step(upper, t_up)
        lower = mean_step(lower, t_low)

    @pl.when(q == GROUP - 1)
    def _():
        e_vec[...] = jnp.zeros((PAD, dim), jnp.float32)

    def take_back(s):
        group_copy(1, 1, s, 1).wait_recv()
        if s == GROUP - 2:
            e_vec[...] = b_got[s]

            @pl.when(jnp.logical_not(high))
            def _():
                group_copy(1, 2, s, 1).wait_recv()
                e_pre[0] = g_got[s]
        else:
            group_copy(1, 2, s, 1).wait_recv()
            e_vec[...] = applied(stacked(e_vec[...]), g_got, s) + b_got[s]

            @pl.when(jnp.logical_not(high))
            def _():
                keep_pre(e_pre, 0, joined(e_pre, 0, g_got, s))

    each_source(1, take_back)

    def settle():
        def sent(t, carry):
            for which in range(2):
                for kind in range(3):
                    move(which, kind, t).wait_send()
            return carry

        lax.fori_loop(0, steps, sent, 0)

        for way, final in ((0, first), (1, last)):

            def done(kind, d):
                group_copy(way, kind, 0, d).wait_send()

            @pl.when(jnp.logical_not(final))
            def _():
                each_target(way, functools.partial(done, 0))

            each_target(way, functools.partial(done, 1))
            each_operator(way, lambda s: group_copy(way, 2, s, 1).wait_send())

    pl.when(low)(settle)

    @pl.when(high)
    def _():
        s_in[...] = e_vec[...]

    @pl.when(jnp.logical_not(high))
    def _():
        chain(1, 1).wait_recv()

        @pl.when(q < GROUP - 1)
        def _():
            s_in[...] = applied(stacked(s_in[...]), e_pre, 0) + e_vec[...]

    returns = jnp.logical_and(q == 0, jnp.logical_not(low))

    @pl.when(last)
    def _():
        smooth_ref[0] = b_out[0:series]
        for t in range(half_steps, steps):
            smooth_ref[t] = lst[t][0:series]

    @pl.when(jnp.logical_not(last))
    def _():
        s = stacked(s_in[...])
        now = applied(s, g_pre, steps) + b_out[...]
        s_out[...] = now
        smooth_ref[0] = now[0:series]

        @pl.when(returns)
        def _():
            for d in reversed(range(1, GROUP + 1)):
                chain(1, d).start()

        for t in range(half_steps, steps):
            now = applied(s, g_pre, t) + lst[t]
            smooth_ref[t] = now[0:series]
            if t == half_steps:
                lst[t] = now

    middle = stacked(lst[half_steps])
    for t in range(1, half_steps):
        smooth_ref[t] = (applied(middle, g_pre, t) + lst[t])[0:series]

    pl.when(jnp.logical_not(low))(settle)

    for way, sender in ((0, gives), (1, returns)):
        @pl.when(sender)
        def _():
            for d in range(1, GROUP + 1):
                chain(way, d).wait_send()


def local(blocks, transition, drive, smoother_gain, dynamics, initial_mean):
    steps, rows, dim = transition.shape
    series = initial_mean.shape[0]
    vmem = pl.BlockSpec(memory_space=pltpu.VMEM)
    hbm = pl.BlockSpec(memory_space=pltpu.HBM)
    full = pltpu.VMEM((steps, dim, dim), jnp.bfloat16)
    a_pre = pltpu.VMEM((steps, 2 * dim + 2 * PAD, dim), jnp.bfloat16)
    g_pre = pltpu.VMEM((steps + 1, 2 * dim, dim), jnp.bfloat16)
    got = pltpu.VMEM((GROUP - 1, 2 * dim, dim), jnp.bfloat16)
    group = pltpu.VMEM((GROUP - 1, PAD, dim), jnp.float32)
    means = pltpu.VMEM((steps, PAD, dim), jnp.float32)
    flat = pltpu.VMEM((steps * PAD, dim), jnp.float32)
    one = pltpu.VMEM((PAD, dim), jnp.float32)
    out = jax.ShapeDtypeStruct(drive.shape, jnp.float32)
    pinned = [
        pltpu.with_memory_space_constraint(x, pltpu.HBM)
        for x in (transition, smoother_gain, drive, dynamics, initial_mean)
    ]
    return pl.pallas_call(
        functools.partial(kernel, blocks, steps, rows, series),
        out_shape=(out, out),
        in_specs=[hbm] * 5,
        out_specs=(vmem, vmem),
        scratch_shapes=[
            pltpu.VMEM(drive.shape, drive.dtype),
            pltpu.VMEM(dynamics.shape, dynamics.dtype),
            pltpu.VMEM(initial_mean.shape, initial_mean.dtype),
            full, full, a_pre, g_pre, got, got, group, group, one, one,
            pltpu.VMEM((1, 2 * dim, dim), jnp.bfloat16), one,
            pltpu.VMEM((1, 2 * dim, dim), jnp.bfloat16), one,
            pltpu.VMEM((steps - 4, 2 * dim, dim), jnp.bfloat16),
            means, flat, means, flat,
            pltpu.VMEM((2, dim, dim), jnp.bfloat16),
            one, one, one, one,
            pltpu.SemaphoreType.DMA((5,)),
            pltpu.SemaphoreType.DMA((2, 3, steps)),
            pltpu.SemaphoreType.DMA((2, 3, steps)),
            pltpu.SemaphoreType.DMA((2, 3, GROUP - 1)),
            pltpu.SemaphoreType.DMA((2, 3, GROUP - 1)),
            pltpu.SemaphoreType.DMA((2, GROUP)),
            pltpu.SemaphoreType.DMA((2,)),
        ],
        compiler_params=pltpu.CompilerParams(
            collective_id=0, has_side_effects=True, vmem_limit_bytes=40 * 1024 * 1024
        ),
    )(*pinned)


def solution(mesh):
    placed = (P("tm", "col", None), P("tm", "col", None), P("tm", "col", None), P(), P("col", None))
    return jax.shard_map(
        functools.partial(local, mesh.shape["tm"]),
        mesh=mesh,
        in_specs=placed,
        out_specs=(P("tm", "col", None), P("tm", "col", None)),
        check_vma=False,
    )
```
